1024 devices in a mesh: region: 32 (over z, core), dom: 32 (over x, y).
Axes of the slice: x: 4, y: 8, z: 16, core: 2. Of those that a mesh axis runs over, the one named last changes fastest.
Arguments:
- positions: float32 [32, 32, 32, 3, 128], P('region', 'dom'), may hold values from -1 to 1
- masses: float32 [32, 32, 32, 128], P('region', 'dom'), may hold values from 0.002 to 0.03
- fill: int32 [32, 32, 32], P('region', 'dom'), may hold values from 1 to 128, 3072 in all within a row
- translations: bfloat16 [165, 21120], replicated, may hold values from -0.0390625 to 0.0390625
- m2l_lists: int32 [32, 32, 32, 128], P('region', 'dom'), may hold values from 0 to 1183, as said below
- cell_sends: int32 [32, 32, 32, 4], P('region', 'dom'), may hold values from 0 to 31
- bin_sends: int32 [32, 32, 32, 1], P('region', 'dom'), may hold values from 0 to 31
- task_target: int32 [32, 32, 128], P('region', 'dom'), may hold values from 0 to 63, as said below
- task_source: int32 [32, 32, 128], P('region', 'dom'), may hold values from 0 to 63, as said below
- task_offset: int32 [32, 32, 128], P('region', 'dom'), may hold values from 0 to 26
Outputs:
- potential: float32 [32, 32, 32, 128], P('region', 'dom')
The draws below stay inside these ranges and needn't reach their ends.
Inputs may be any that keep to these rules, and one draw needn't show every extreme that they name: `m2l_lists`: each entry names a row of the domain's source_table: a top cell below 1024, then a received cell, then an own bin. Every received cell is named by some entry of the domain. `task_target`: an index below 32 is an own bin, the others name the 32 received bins sender by sender. Every received bin is the target of some task of the domain and the source of some other. `task_source`: indexed as task_target; every received bin is the source of some task.
All inputs are finite; a program needn't handle non-finite values.
Results may differ from the reference program's by a relative error of at most 0.0016.
Values may be sent and summed in bfloat16 or wider, within the bound.
No kernel may reach another device: no remote copies, remote signals or barrier semaphores. Data moves between devices by JAX's collectives and lax.ppermute only.
A program may use at most 64 MiB of HBM per device.

```python
import math
import jax
import jax.numpy as jnp
import numpy as np
from jax import lax

ORDER = 8
NC = 165
P_SIZE = 128
NB = 32
KL = 128
SEND = 4
SB = 1
TASK_DEV = 128
N_REGION = 32
N_DOM = 32


def task_plan(key):
    plan_key = jax.random.fold_in(key, 11)
    domains = N_REGION * N_DOM
    received = N_DOM * SB
    keys_all = jax.random.split(plan_key, 7)
    slot_ids = jnp.arange(TASK_DEV, dtype=jnp.int32)
    kind = slot_ids % 4
    quarter = slot_ids // 4 % received
    cover_first = jax.vmap(lambda part_key: jax.random.permutation(part_key, received))(jax.random.split(keys_all[0], domains))
    cover_second = jax.vmap(lambda part_key: jax.random.permutation(part_key, received))(jax.random.split(keys_all[1], domains))
    pick_first = cover_first[:, quarter].astype(jnp.int32) + NB
    pick_second = cover_second[:, quarter].astype(jnp.int32) + NB
    own_target = jax.random.randint(keys_all[2], (domains, TASK_DEV), 0, NB)
    own_source = jax.random.randint(keys_all[3], (domains, TASK_DEV), 0, NB)
    far_target = jax.random.randint(keys_all[4], (domains, TASK_DEV), NB, NB + received)
    far_source = jax.random.randint(keys_all[5], (domains, TASK_DEV), NB, NB + received)
    targets = jnp.where(kind == 0, own_target, jnp.where(kind == 1, pick_second, jnp.where(kind == 2, own_target, far_target)))
    sources = jnp.where(kind == 0, pick_first, jnp.where(kind == 1, own_source, jnp.where(kind == 2, own_source, far_source)))
    shuffle = jax.vmap(lambda part_key: jax.random.permutation(part_key, TASK_DEV))(jax.random.split(keys_all[6], domains))
    targets = jnp.take_along_axis(targets, shuffle, axis=1).astype(jnp.int32)
    sources = jnp.take_along_axis(sources, shuffle, axis=1).astype(jnp.int32)
    return (targets.reshape(N_REGION, N_DOM, TASK_DEV), sources.reshape(N_REGION, N_DOM, TASK_DEV))


def draw_task_target(key, part):
    shared = task_plan(key)
    return shared[0]


def draw_task_source(key, part):
    shared = task_plan(key)
    return shared[1]


def draw_m2l_lists(key, part):
    key = jax.random.fold_in(key, 5)
    domains = N_REGION * N_DOM
    tops = N_REGION * N_DOM
    rcells = N_DOM * SEND
    top_cols = KL * 3 // 8
    cell_cols = KL * 3 // 8
    own_cols = KL - top_cols - cell_cols
    keys_all = jax.random.split(key, 4)
    top_pick = jax.random.randint(keys_all[0], (domains, NB, top_cols), 0, tops)
    cover = jax.vmap(lambda part_key: jax.random.permutation(part_key, rcells))(jax.random.split(keys_all[1], domains))
    spots = (jnp.arange(NB, dtype=jnp.int32)[:, None] * cell_cols + jnp.arange(cell_cols, dtype=jnp.int32)[None, :]) % rcells
    cell_pick = tops + cover[:, spots].astype(jnp.int32)
    own_pick = tops + rcells + jax.random.randint(keys_all[2], (domains, NB, own_cols), 0, NB)
    entries = jnp.concatenate([top_pick, cell_pick, own_pick], axis=-1)
    shuffle = jax.vmap(lambda part_key: jax.random.permutation(part_key, KL))(jax.random.split(keys_all[3], domains * NB))
    entries = jnp.take_along_axis(entries, shuffle.reshape(domains, NB, KL), axis=-1)
    return entries.astype(jnp.int32).reshape(N_REGION, N_DOM, NB, KL)


def set_ends(values, own_key, least, top_value):
    longest = values.shape.index(max(values.shape))
    spots = []
    for shift in (0, 1):
        where = [jax.random.randint(jax.random.fold_in(own_key, axis), (), 0, length) for axis, length in enumerate(values.shape)]
        where[longest] = (where[longest] + shift) % values.shape[longest]
        spots.append(tuple(where))
    return values.at[spots[0]].set(least).at[spots[1]].set(top_value)


def steps_of(stream_key, shape, shards, least, largest):
    gain, own = 1.0, jax.random.fold_in(stream_key, 6)
    for dim, blocks in shards:
        steps = jnp.exp(jax.random.uniform(jax.random.fold_in(own, dim), (blocks,), jnp.float32, least / len(shards), largest / len(shards)))
        gain = gain * jnp.repeat(steps, shape[dim] // blocks).reshape([-1 if axis == dim else 1 for axis in range(len(shape))])
    return gain


def length_profile(amount, total, most, lean):
    portions = [(1 << 20) // math.isqrt(standing ** lean) + 1 for standing in range(2, amount + 1)]
    spare, holding = total - most - (amount - 1), [1] * (amount - 1)
    while spare > 0:
        movable = [i for i in range(amount - 1) if holding[i] < most]
        pool, remaining = sum([portions[i] for i in movable]), spare
        for i in movable:
            extra = min(most - holding[i], max(1, remaining * portions[i] // pool), spare)
            holding[i] = holding[i] + extra
            spare = spare - extra
    return np.array([most] + holding)


def uneven_parts(key, amount, total, most, skew):
    if amount == 2:
        one = jax.random.randint(key, (), max(1, total - most), min(most, total - 1) + 1)
        return jnp.stack([one, total - one])
    sizes = jnp.asarray(length_profile(amount, total, most, skew), jnp.int32)
    pairs = (amount - 1) // 2
    source_of, receiver = sizes[1:1 + 2 * pairs:2], sizes[2:2 + 2 * pairs:2]
    margin = jnp.minimum(source_of - 1, most - receiver)
    passed = jax.random.randint(jax.random.fold_in(key, 1), (pairs,), 0, 1 << 20) % (margin + 1)
    sizes = sizes.at[1:1 + 2 * pairs:2].set(source_of - passed).at[2:2 + 2 * pairs:2].set(receiver + passed)
    return sizes[jax.random.permutation(jax.random.fold_in(key, 2), amount)]


def normal_values(stream_key, extent, deviation, most, held_as=jnp.bfloat16):
    drawn = jax.random.normal(stream_key, extent, jnp.float32) * deviation
    return jnp.minimum(jnp.maximum(drawn, -most), most).astype(held_as)


def setup_inputs(seed: int = 0) -> dict:
    key_list = jax.random.split(jax.random.key(seed), 11)
    return {
        "positions": jnp.clip(jax.random.uniform(key_list[0], (N_REGION, N_DOM, NB, 3, P_SIZE), jnp.float32, -1.0, 1.0) * steps_of(key_list[0], (N_REGION, N_DOM, NB, 3, P_SIZE), ((0, 32), (1, 32)), -0.4, 0.0), -1.0, 1.0),
        "masses": jnp.clip(jnp.exp(math.log(0.03) - 2.70805 * jax.random.uniform(key_list[1], (N_REGION, N_DOM, NB, P_SIZE), jnp.float32) ** steps_of(key_list[1], (N_REGION, N_DOM, NB, P_SIZE), ((0, 32), (1, 32)), -0.2, 0.2)), 0.002, 0.03),
        "fill": jax.vmap(lambda own: uneven_parts(own, NB, NB * P_SIZE * 3 // 4, P_SIZE, 2))(jax.random.split(key_list[2], N_REGION * N_DOM)).reshape((N_REGION, N_DOM, NB)).astype(jnp.int32),
        "translations": normal_values(key_list[3], (NC, KL * NC), (NC * KL) ** -0.5, 0.0390625),
        "m2l_lists": draw_m2l_lists(jax.random.fold_in(key_list[10], 71), 0),
        "cell_sends": set_ends(jax.random.randint(key_list[5], (N_REGION, N_DOM, N_DOM, SEND), 0, NB), jax.random.fold_in(key_list[5], 1), 0, NB - 1).astype(jnp.int32),
        "bin_sends": set_ends(jax.random.randint(key_list[6], (N_REGION, N_DOM, N_DOM, SB), 0, NB), jax.random.fold_in(key_list[6], 1), 0, NB - 1).astype(jnp.int32),
        "task_target": draw_task_target(jax.random.fold_in(key_list[10], 71), 0),
        "task_source": draw_task_source(jax.random.fold_in(key_list[10], 71), 0),
        "task_offset": set_ends(jax.random.randint(key_list[9], (N_REGION, N_DOM, TASK_DEV), 0, 27), jax.random.fold_in(key_list[9], 1), 0, 26).astype(jnp.int32),
    }


SOFTENING = 0.01
HIGHEST = lax.Precision.HIGHEST

def exponent_table(order):
    triples = []
    for degree_sum in range(order + 1):
        for first_power in range(degree_sum, -1, -1):
            for second_power in range(degree_sum - first_power, -1, -1):
                triples.append((first_power, second_power, degree_sum - first_power - second_power))
    return np.array(triples, dtype=np.int32).T

def leaf_basis(points, order):
    series = [jnp.ones_like(points), points]
    for degree in range(2, order + 1):
        series.append(2.0 * points * series[-1] - series[-2])
    chebyshev = jnp.stack(series[:order + 1], axis=0)
    powers = exponent_table(order)
    values = chebyshev[powers[0], :, 0, :] * chebyshev[powers[1], :, 1, :] * chebyshev[powers[2], :, 2, :]
    return jnp.transpose(values, (1, 0, 2))

def pair_potential(target_points, source_points, source_masses, offset, same_bin):
    shift = 2.0 * jnp.stack([offset // 9 - 1, offset // 3 % 3 - 1, offset % 3 - 1]).astype(jnp.float32)
    delta = source_points[:, None, :] + shift[:, None, None] - target_points[:, :, None]
    distance = lax.optimization_barrier(jnp.sum(delta * delta, axis=0)) + SOFTENING
    weight = source_masses[None, :] / jnp.sqrt(distance)
    slots = target_points.shape[-1]
    keep = jnp.logical_not(jnp.logical_and(same_bin, jnp.eye(slots, dtype=bool)))
    return lax.optimization_barrier(jnp.sum(jnp.where(keep, weight, 0.0), axis=1))

def pick_rows(table_rows, picked_ids):
    return table_rows[picked_ids]

def device_near(device_args):
    all_points, all_masses, targets, sources, offsets = device_args

    def one_task(target_id, source_id, offset):
        same_bin = jnp.logical_and(target_id == source_id, offset == 13)
        return pair_potential(all_points[target_id], all_points[source_id], all_masses[source_id], offset, same_bin)
    task_values = jax.vmap(one_task)(targets, sources, offsets)
    placing = (jnp.arange(all_points.shape[0], dtype=jnp.int32)[:, None] == targets[None, :]).astype(jnp.float32)
    return jnp.dot(placing, task_values, precision=HIGHEST)

def reference(positions, masses, fill, translations, m2l_lists, cell_sends, bin_sends, task_target, task_source, task_offset):
    devices = N_REGION * N_DOM
    live = jnp.arange(P_SIZE, dtype=jnp.int32)[None, None, None, :] < fill[..., None]
    live_mass = jnp.where(live, masses, 0.0)

    def region_moments(region_args):
        region_points, region_masses = region_args
        basis = leaf_basis(region_points.reshape(-1, 3, P_SIZE), ORDER).reshape(N_DOM, NB, -1, P_SIZE)
        return jnp.einsum('dbcp,dbp->dbc', basis, region_masses, precision=HIGHEST)
    moments = lax.map(region_moments, (positions, live_mass))
    leaf_moments = moments.astype(jnp.bfloat16)
    top_table = lax.optimization_barrier(jnp.mean(moments, axis=2)).astype(jnp.bfloat16).reshape(devices, -1)
    coeffs = top_table.shape[1]
    wide_ops = translations.astype(jnp.float32).reshape(coeffs, KL, coeffs)

    def region_work(region_args):
        region_points, region_masses, region_leaf, region_lists, region_cells, region_bins, region_targets, region_sources, region_offsets = region_args
        sent = jax.vmap(pick_rows)(region_leaf, region_cells)
        incoming = jnp.transpose(sent, (1, 0, 2, 3)).reshape(N_DOM, -1, coeffs)
        source_table = jnp.concatenate([jnp.broadcast_to(top_table[None], (N_DOM,) + top_table.shape), incoming, region_leaf], axis=1)
        picked = jax.vmap(pick_rows)(source_table, region_lists)
        local = jnp.einsum('dbkc,akc->dba', picked.astype(jnp.float32), wide_ops, precision=HIGHEST)
        basis = leaf_basis(region_points.reshape(-1, 3, P_SIZE), ORDER).reshape(N_DOM, NB, -1, P_SIZE)
        far = jnp.einsum('dba,dbap->dbp', local, basis, precision=HIGHEST)
        moved_points = jax.vmap(pick_rows)(region_points, region_bins)
        moved_points = jnp.transpose(moved_points, (1, 0, 2, 3, 4)).reshape(N_DOM, -1, 3, P_SIZE)
        moved_masses = jax.vmap(pick_rows)(region_masses, region_bins)
        moved_masses = jnp.transpose(moved_masses, (1, 0, 2, 3)).reshape(N_DOM, -1, P_SIZE)
        all_points = jnp.concatenate([region_points, moved_points], axis=1)
        all_masses = jnp.concatenate([region_masses, moved_masses], axis=1)
        near = lax.map(device_near, (all_points, all_masses, region_targets, region_sources, region_offsets))
        back = near[:, NB:].reshape(N_DOM, N_DOM, SB, P_SIZE)
        homing = (region_bins[:, :, :, None] == jnp.arange(NB, dtype=jnp.int32)[None, None, None, :]).astype(jnp.float32)
        home = jnp.einsum('oejb,eojp->obp', homing, back, precision=HIGHEST)
        return far + near[:, :NB] + home
    total = lax.map(region_work, (positions, live_mass, leaf_moments, m2l_lists, cell_sends, bin_sends, task_target, task_source, task_offset))
    return jnp.where(live, total, 0.0)
```

```python
import functools
import jax
import jax.numpy as jnp
import numpy as np
from jax import lax
from jax.experimental import pallas as pl
from jax.experimental.pallas import tpu as pltpu
from jax.sharding import PartitionSpec as P

ORDER = 8
SOFTENING = 0.01
LANES = 128
WIDTH = 256
SLOTS = 64
F32 = jnp.float32
BF16 = jnp.bfloat16
VMEM = pl.BlockSpec(memory_space=pltpu.VMEM)
SMEM = pl.BlockSpec(memory_space=pltpu.SMEM)


def coefficient_groups():
    groups = []
    for ax in range(ORDER + 1):
        for ay in range(ORDER + 1 - ax):
            for part in range((ORDER - ax - ay) // 4 + 1):
                groups.append((ax, ay, part))
    return groups


GROUPS = coefficient_groups()


def placing_matrix():
    index, at = {}, 0
    for total in range(ORDER + 1):
        for ax in range(total, -1, -1):
            for ay in range(total - ax, -1, -1):
                index[(ax, ay, total - ax - ay)] = at
                at += 1
    placing = np.zeros((WIDTH, WIDTH), np.float32)
    for row, (ax, ay, part) in enumerate(GROUPS):
        for j in range(4):
            place = index.get((ax, ay, 4 * part + j))
            if place is not None:
                placing[j * SLOTS + row, place] = 1.0
    return placing


def chebyshev(t):
    series = [jnp.ones_like(t), t]
    for _ in range(2, ORDER + 1):
        series.append(2.0 * t * series[-1] - series[-2])
    return series


def grouped(series, lane_group):
    parts = []
    for n in range(3):
        value = series[4 * n]
        for j in range(1, 4):
            other = series[4 * n + j] if 4 * n + j <= ORDER else jnp.zeros_like(value)
            value = jnp.where(lane_group == j, other, value)
        parts.append(value)
    return parts


def four_wide(rows):
    return jnp.concatenate([rows] * 4, axis=0).T


def live_rows(fill_row, masses):
    bins, slots = masses.shape
    eye = lax.broadcasted_iota(jnp.int32, (bins, bins), 0) == lax.broadcasted_iota(
        jnp.int32, (bins, bins), 1
    )
    fill_col = jnp.sum(
        jnp.where(eye, fill_row.astype(F32), 0.0), axis=1, keepdims=True
    )
    slot = lax.broadcasted_iota(jnp.int32, (bins, slots), 1).astype(F32)
    return slot < fill_col


def moments_kernel(pos, mass, fill, cells, sends, placing, leaf_out, live_out, top_out, cast_out, acc, wide):
    bins = mass.shape[0]
    live_mass = jnp.where(live_rows(fill[...], mass[...]), mass[...], 0.0)
    live_out[...] = live_mass
    for c in range(3):
        wide[c] = four_wide(pos[c])
    wide[3] = four_wide(live_mass)
    acc[...] = jnp.zeros_like(acc)
    lane_group = lax.div(lax.broadcasted_iota(jnp.int32, (8, LANES), 1), bins)

    def step(i, carry):
        sums = [None] * len(GROUPS)
        for half in range(2):
            rows = pl.ds(pl.multiple_of(16 * i + 8 * half, 8), 8)
            tx = chebyshev(wide[0, rows, :])
            ty = chebyshev(wide[1, rows, :])
            m = wide[3, rows, :]
            tz = [v * m for v in grouped(chebyshev(wide[2, rows, :]), lane_group)]
            last = None
            for g, (ax, ay, part) in enumerate(GROUPS):
                if last is None or last[0] != (ax, ay):
                    last = ((ax, ay), tx[ax] * ty[ay] if ax and ay else (tx[ax] if ax else ty[ay]))
                value = last[1] * tz[part] if (ax or ay) else tz[part]
                sums[g] = value if sums[g] is None else sums[g] + value
        for g in range(len(GROUPS)):
            acc[g] += sums[g]
        return carry

    lax.fori_loop(0, 8, step, 0)
    raw = jnp.sum(acc[...], axis=1).T
    moments = jnp.concatenate([raw[bins * j : bins * (j + 1)] for j in range(4)], axis=1)
    top = jnp.sum(moments, axis=0, keepdims=True) * (1.0 / bins)
    both = jnp.concatenate([moments, jnp.broadcast_to(top, (bins, WIDTH))], axis=0).astype(BF16)
    placed = jnp.dot(both, placing[...], preferred_element_type=F32)
    leaf = placed[:bins].astype(BF16)
    leaf_out[...] = leaf
    top_out[:, 0, :] = placed[bins:, :LANES]
    top_out[:, 1, :] = placed[bins:, LANES:]
    doms = cells.shape[1]
    for s in range(cells.shape[0]):
        pick = (lax.broadcasted_iota(jnp.int32, (bins, doms), 0) == cells[s : s + 1, :]).astype(F32).astype(BF16)
        one = lax.dot_general(pick, leaf, (((0,), (0,)), ((), ())), preferred_element_type=F32)
        cast_out[:, 4 + 2 * s, :] = one[:, :LANES]
        cast_out[:, 5 + 2 * s, :] = one[:, LANES:]
    for d in range(doms):
        b = sends[d]
        for c in range(3):
            cast_out[d, c : c + 1, :] = pos[c, pl.ds(b, 1), :]
        cast_out[d, 3:4, :] = live_out[pl.ds(b, 1), :]
        cast_out[d, 12:16, :] = jnp.zeros((4, LANES), F32)


def moments_call(pos, mass, fill, cells, sends, placing):
    bins, doms = mass.shape[0], cells.shape[1]
    return pl.pallas_call(
        moments_kernel,
        out_shape=(
            jax.ShapeDtypeStruct((bins, WIDTH), BF16),
            jax.ShapeDtypeStruct((bins, LANES), F32),
            jax.ShapeDtypeStruct((bins, 2, LANES), F32),
            jax.ShapeDtypeStruct((doms, 16, LANES), F32),
        ),
        in_specs=[VMEM] * 4 + [SMEM, VMEM],
        out_specs=(VMEM,) * 4,
        scratch_shapes=[
            pltpu.VMEM((SLOTS, 8, LANES), F32),
            pltpu.VMEM((4, LANES, LANES), F32),
        ],
        cost_estimate=pl.CostEstimate(flops=6_000_000, bytes_accessed=600_000, transcendentals=0),
        name="moments",
    )(pos, mass, fill, cells, sends, placing)


def spread_kernel(tops, out):
    both = jnp.concatenate([tops[:, 0, :], tops[:, 1, :]], axis=1).astype(BF16)
    for d in range(out.shape[0]):
        out[d] = both


def spread_call(tops, doms):
    return pl.pallas_call(
        spread_kernel,
        out_shape=jax.ShapeDtypeStruct((doms, tops.shape[0], WIDTH), BF16),
        in_specs=[VMEM],
        out_specs=VMEM,
        cost_estimate=pl.CostEstimate(flops=0, bytes_accessed=600_000, transcendentals=0),
        name="spread",
    )(tops)


def near_kernel(pos, live_mass, got, target, source, offset, near_out, back_out, rows, cols, acc):
    own = live_mass.shape[0]
    total = rows.shape[0]
    for c in range(3):
        rows[:own, c, :] = pos[c]
    rows[:own, 3, :] = live_mass[...]
    rows[own:, 0:4, :] = got[:, 0:4, :]
    rows[:, 4:, :] = jnp.zeros((total, 4, LANES), F32)
    acc[...] = jnp.zeros_like(acc)

    def turn(b, carry):
        cols[b, :, 0:8] = rows[b].T
        return carry

    lax.fori_loop(0, total, turn, 0, unroll=4)

    def task(t, carry):
        i, j, o = target[t], source[t], offset[t]
        sx = 2.0 * (lax.div(o, 9) - 1).astype(F32)
        sy = 2.0 * (lax.rem(lax.div(o, 3), 3) - 1).astype(F32)
        sz = 2.0 * (lax.rem(o, 3) - 1).astype(F32)
        tx = rows[i, 0:1, :] - sx
        ty = rows[i, 1:2, :] - sy
        tz = rows[i, 2:3, :] - sz

        def sweep(skip_self):
            parts = []
            for n in range(LANES // 8):
                part = cols[j, 8 * n : 8 * n + 8, :]
                dx = part[:, 0:1] - tx
                dy = part[:, 1:2] - ty
                dz = part[:, 2:3] - tz
                d = (dx * dx + SOFTENING) + dy * dy + dz * dz
                w = part[:, 3:4] * lax.rsqrt(d)
                if skip_self:
                    q = lax.broadcasted_iota(jnp.int32, (8, LANES), 0) + 8 * n
                    p = lax.broadcasted_iota(jnp.int32, (8, LANES), 1)
                    w = jnp.where(p == q, 0.0, w)
                parts.append(w)
            while len(parts) > 1:
                parts = [a + b for a, b in zip(parts[::2], parts[1::2])]
            acc[i] += parts[0]

        same = jnp.logical_and(i == j, o == 13)

        @pl.when(same)
        def _():
            sweep(True)

        @pl.when(jnp.logical_not(same))
        def _():
            sweep(False)

        return carry

    lax.fori_loop(0, target.shape[0], task, 0)
    near = jnp.sum(acc[...], axis=1)
    near_out[...] = near[:own]
    back_out[...] = near[own:]


def near_call(pos, live_mass, got, target, source, offset):
    own = live_mass.shape[0]
    total = own + got.shape[0]
    return pl.pallas_call(
        near_kernel,
        out_shape=(jax.ShapeDtypeStruct((own, LANES), F32), jax.ShapeDtypeStruct((total - own, LANES), F32)),
        in_specs=[VMEM, VMEM, VMEM, SMEM, SMEM, SMEM],
        out_specs=(VMEM, VMEM),
        cost_estimate=pl.CostEstimate(flops=26_000_000, bytes_accessed=600_000, transcendentals=2_000_000),
        scratch_shapes=[
            pltpu.VMEM((total, 8, LANES), F32),
            pltpu.VMEM((total, LANES, LANES), F32),
            pltpu.VMEM((total, 8, LANES), F32),
        ],
        compiler_params=pltpu.CompilerParams(vmem_limit_bytes=24 * 2**20),
        name="near",
    )(pos, live_mass, got, target, source, offset)


def widen_kernel(ops, wide_out):
    coeffs = ops.shape[0]
    for n in range(wide_out.shape[0]):
        first = n * coeffs
        base = first // LANES * LANES
        stop = min(base + 3 * LANES, ops.shape[1])
        part = ops[:, base:stop][:, first - base : first - base + coeffs]
        wide_out[n, :coeffs, :coeffs] = part
        wide_out[n, :coeffs, coeffs:] = jnp.zeros((coeffs, WIDTH - coeffs), BF16)


def widen_call(ops):
    coeffs = ops.shape[0]
    entries = ops.shape[1] // coeffs
    return pl.pallas_call(
        widen_kernel,
        out_shape=jax.ShapeDtypeStruct((entries, coeffs, WIDTH), BF16),
        in_specs=[VMEM],
        out_specs=VMEM,
        compiler_params=pltpu.CompilerParams(vmem_limit_bytes=40 * 2**20),
        cost_estimate=pl.CostEstimate(flops=0, bytes_accessed=18_000_000, transcendentals=0),
        name="widen",
    )(ops)


def final_kernel(mode, top, got, leaf, lists, ops, placing, pos, mass, fill, near, back, sends,
                 out, table, far_cols, local_rows, homes):
    bins, entries = lists.shape
    tops = top.shape[0]
    doms = got.shape[0]
    sent = 4
    for s in range(sent):
        table[tops + doms * s : tops + doms * (s + 1), :LANES] = got[:, 4 + 2 * s, :].astype(BF16)
        table[tops + doms * s : tops + doms * (s + 1), LANES:] = got[:, 5 + 2 * s, :].astype(BF16)
    used = tops + doms * sent
    table[used : used + bins] = leaf[...]
    used += bins
    table[:tops] = top[...]
    ids = lists[...]
    regions = tops // doms
    cell = ids - tops
    ids = jnp.where(
        ids < tops,
        (ids & (doms - 1)) * regions + lax.div(ids, doms),
        jnp.where(cell < doms * sent, tops + (cell & (sent - 1)) * doms + lax.div(cell, sent), ids),
    )
    table[used:] = jnp.zeros((table.shape[0] - used, WIDTH), BF16)
    rows = lax.broadcasted_iota(jnp.int32, (bins, table.shape[0]), 1)
    local = None
    for n in range(0, entries, 8):
        pick = jnp.concatenate(
            [(ids[:, k : k + 1] == rows).astype(F32).astype(BF16) for k in range(n, n + 8)], axis=0
        )
        picked = jnp.dot(pick, table[...], preferred_element_type=F32).astype(BF16)
        for k in range(8):
            one = picked[bins * k : bins * (k + 1)]
            if mode == 0:
                term = lax.dot_general(one, ops[n + k], (((1,), (1,)), ((), ())), preferred_element_type=F32)
            else:
                term = lax.dot_general(ops[n + k], one, (((1,), (1,)), ((), ())), preferred_element_type=F32)
            local = term if local is None else local + term
    pad = jnp.zeros((bins, WIDTH - ops.shape[1]), F32) if mode == 0 else jnp.zeros((WIDTH - ops.shape[1], bins), F32)
    local = jnp.concatenate([local, pad], axis=1 if mode == 0 else 0)
    spread = None
    rest = local
    for _ in range(3):
        piece = rest.astype(BF16)
        rest = rest - piece.astype(F32)
        dims = (((1,), (1,)), ((), ())) if mode == 0 else (((1,), (0,)), ((), ()))
        term = lax.dot_general(placing[...], piece, dims, preferred_element_type=F32)
        spread = term if spread is None else spread + term
    local_rows[...] = jnp.concatenate([spread[SLOTS * j : SLOTS * (j + 1)] for j in range(4)], axis=1)
    lane_group = lax.div(lax.broadcasted_iota(jnp.int32, (8, LANES), 1), bins)
    wide = far_cols
    for c in range(3):
        wide[c] = four_wide(pos[c])

    def step(i, carry):
        series = []
        for half in range(2):
            at = pl.ds(pl.multiple_of(16 * i + 8 * half, 8), 8)
            tx = chebyshev(wide[0, at, :])
            ty = chebyshev(wide[1, at, :])
            tz = grouped(chebyshev(wide[2, at, :]), lane_group)
            series.append((at, tx, ty, tz))
        totals = [None, None]
        g = 0
        while g < len(GROUPS):
            ax, ay, _ = GROUPS[g]
            inner = [None, None]
            while g < len(GROUPS) and GROUPS[g][:2] == (ax, ay):
                row = local_rows[g : g + 1, :]
                for h in range(2):
                    value = series[h][3][GROUPS[g][2]] * row
                    inner[h] = value if inner[h] is None else inner[h] + value
                g += 1
            for h in range(2):
                _, tx, ty, _ = series[h]
                value = inner[h]
                if ax:
                    value = value * tx[ax]
                if ay:
                    value = value * ty[ay]
                totals[h] = value if totals[h] is None else totals[h] + value
        for h in range(2):
            wide[3, series[h][0], :] = totals[h]
        return carry

    lax.fori_loop(0, 8, step, 0)
    spread_far = wide[3].T
    far = spread_far[:bins]
    for j in range(1, 4):
        far = far + spread_far[bins * j : bins * (j + 1)]
    homes[...] = far + near[...]
    for d in range(back.shape[0]):
        homes[pl.ds(sends[d], 1), :] += back[d : d + 1, :]
    out[...] = jnp.where(live_rows(fill[...], mass[...]), homes[...], 0.0)


def final_call(top, got, leaf, lists, ops, placing, pos, mass, fill, near, back, sends, mode=0):
    bins, slots = mass.shape
    table_rows = -(-(top.shape[0] + 4 * got.shape[0] + bins) // 256) * 256
    return pl.pallas_call(
        functools.partial(final_kernel, mode),
        out_shape=jax.ShapeDtypeStruct((bins, slots), F32),
        in_specs=[VMEM] * 11 + [SMEM],
        out_specs=VMEM,
        scratch_shapes=[
            pltpu.VMEM((table_rows, WIDTH), BF16),
            pltpu.VMEM((4, LANES, LANES), F32),
            pltpu.VMEM((SLOTS, LANES), F32),
            pltpu.VMEM((bins, slots), F32),
        ],
        compiler_params=pltpu.CompilerParams(vmem_limit_bytes=40 * 2**20),
        cost_estimate=pl.CostEstimate(flops=5_000_000_000, bytes_accessed=12_000_000, transcendentals=0),
        name="final",
    )(top, got, leaf, lists, ops, placing, pos, mass, fill, near, back, sends)


def shards(positions, masses, fill, translations, m2l_lists, cell_sends, bin_sends, task_target, task_source, task_offset):
    pos = jnp.transpose(positions[0, 0], (1, 0, 2))
    mass = masses[0, 0]
    fill_row = fill[0]
    cells = cell_sends[0, 0].T
    sends = bin_sends.reshape(-1)
    placing = jnp.asarray(placing_matrix(), BF16)
    doms = cells.shape[1]
    leaf, live_mass, top_rows, cast = moments_call(pos, mass, fill_row, cells, sends, placing)
    column = lax.all_to_all(top_rows, "region", split_axis=0, concat_axis=0, tiled=True)
    got = lax.all_to_all(cast, "dom", split_axis=0, concat_axis=0, tiled=True)
    wide = widen_call(translations)
    tops = lax.all_to_all(spread_call(column, doms), "dom", split_axis=0, concat_axis=0, tiled=True)
    near, back = near_call(pos, live_mass, got, task_target.reshape(-1), task_source.reshape(-1), task_offset.reshape(-1))
    returned = lax.all_to_all(back.reshape(doms, 1, LANES), "dom", split_axis=0, concat_axis=0, tiled=True)
    out = final_call(
        tops.reshape(-1, WIDTH), got, leaf, m2l_lists[0, 0], wide, placing, pos, mass, fill_row, near,
        returned.reshape(doms, LANES), sends,
    )
    return out[None, None]


def solution(mesh):
    return jax.shard_map(
        shards,
        mesh=mesh,
        in_specs=(
            P("region", "dom", None, None, None),
            P("region", "dom", None, None),
            P("region", "dom", None),
            P(),
            P("region", "dom", None, None),
            P("region", "dom", None, None),
            P("region", "dom", None, None),
            P("region", "dom", None),
            P("region", "dom", None),
            P("region", "dom", None),
        ),
        out_specs=P("region", "dom", None, None),
        check_vma=False,
    )
```

```python
import functools
import jax
import jax.numpy as jnp
import numpy as np
from jax import lax
from jax.experimental import pallas as pl
from jax.experimental.pallas import tpu as pltpu
from jax.sharding import PartitionSpec as P

ORDER = 8
SOFTENING = 0.01
LANES = 128
WIDTH = 256
PIECES = 5
SENT = 4
SLOTS = 64
F32 = jnp.float32
BF16 = jnp.bfloat16
VMEM = pl.BlockSpec(memory_space=pltpu.VMEM)
HBM = pl.BlockSpec(memory_space=pltpu.HBM)
SMEM = pl.BlockSpec(memory_space=pltpu.SMEM)


def coefficient_groups():
    groups = []
    for ax in range(ORDER + 1):
        for ay in range(ORDER + 1 - ax):
            for part in range((ORDER - ax - ay) // 4 + 1):
                groups.append((ax, ay, part))
    return groups


GROUPS = coefficient_groups()


def placing_matrix():
    index, at = {}, 0
    for total in range(ORDER + 1):
        for ax in range(total, -1, -1):
            for ay in range(total - ax, -1, -1):
                index[(ax, ay, total - ax - ay)] = at
                at += 1
    placing = np.zeros((WIDTH, WIDTH), np.float32)
    for row, (ax, ay, part) in enumerate(GROUPS):
        for j in range(4):
            place = index.get((ax, ay, 4 * part + j))
            if place is not None:
                placing[j * SLOTS + row, place] = 1.0
    return placing


def chebyshev(t):
    series = [jnp.ones_like(t), t]
    for _ in range(2, ORDER + 1):
        series.append(2.0 * t * series[-1] - series[-2])
    return series


def grouped(series, lane_group):
    parts = []
    for n in range(3):
        value = series[4 * n]
        for j in range(1, 4):
            other = series[4 * n + j] if 4 * n + j <= ORDER else jnp.zeros_like(value)
            value = jnp.where(lane_group == j, other, value)
        parts.append(value)
    return parts


def four_wide(rows):
    return jnp.concatenate([rows] * 4, axis=0).T


def live_rows(fill_row, masses):
    bins, slots = masses.shape
    eye = lax.broadcasted_iota(jnp.int32, (bins, bins), 0) == lax.broadcasted_iota(
        jnp.int32, (bins, bins), 1
    )
    fill_col = jnp.sum(
        jnp.where(eye, fill_row.astype(F32), 0.0), axis=1, keepdims=True
    )
    slot = lax.broadcasted_iota(jnp.int32, (bins, slots), 1).astype(F32)
    return slot < fill_col


def moments_kernel(pos, mass, fill, cells, sends, placing, leaf_out, live_out, cast_out, acc, wide):
    bins = mass.shape[0]
    live_mass = jnp.where(live_rows(fill[...], mass[...]), mass[...], 0.0)
    live_out[...] = live_mass
    for c in range(3):
        wide[c] = four_wide(pos[c])
    wide[3] = four_wide(live_mass)
    acc[...] = jnp.zeros_like(acc)
    lane_group = lax.div(lax.broadcasted_iota(jnp.int32, (8, LANES), 1), bins)

    def step(i, carry):
        sums = [None] * len(GROUPS)
        for half in range(2):
            rows = pl.ds(pl.multiple_of(16 * i + 8 * half, 8), 8)
            tx = chebyshev(wide[0, rows, :])
            ty = chebyshev(wide[1, rows, :])
            m = wide[3, rows, :]
            tz = [v * m for v in grouped(chebyshev(wide[2, rows, :]), lane_group)]
            last = None
            for g, (ax, ay, part) in enumerate(GROUPS):
                if last is None or last[0] != (ax, ay):
                    last = ((ax, ay), tx[ax] * ty[ay] if ax and ay else (tx[ax] if ax else ty[ay]))
                value = last[1] * tz[part] if (ax or ay) else tz[part]
                sums[g] = value if sums[g] is None else sums[g] + value
        for g in range(len(GROUPS)):
            acc[g] += sums[g]
        return carry

    lax.fori_loop(0, 8, step, 0)
    raw = jnp.sum(acc[...], axis=1).T
    moments = jnp.concatenate([raw[bins * j : bins * (j + 1)] for j in range(4)], axis=1)
    top = jnp.sum(moments, axis=0, keepdims=True) * (1.0 / bins)
    both = jnp.concatenate([moments, jnp.broadcast_to(top, (cells.shape[1], WIDTH))], axis=0).astype(BF16)
    placed = jnp.dot(both, placing[...], preferred_element_type=F32)
    leaf = placed[:bins].astype(BF16)
    leaf_out[...] = leaf
    doms = cells.shape[1]
    cast_out[:, 12, :] = placed[bins:, :LANES]
    cast_out[:, 13, :] = placed[bins:, LANES:]
    for s in range(cells.shape[0]):
        pick = (lax.broadcasted_iota(jnp.int32, (bins, doms), 0) == cells[s : s + 1, :]).astype(F32).astype(BF16)
        one = lax.dot_general(pick, leaf, (((0,), (0,)), ((), ())), preferred_element_type=F32)
        cast_out[:, 4 + 2 * s, :] = one[:, :LANES]
        cast_out[:, 5 + 2 * s, :] = one[:, LANES:]
    for d in range(doms):
        b = sends[0, d]
        for c in range(3):
            cast_out[d, c : c + 1, :] = pos[c, pl.ds(b, 1), :]
        cast_out[d, 3:4, :] = live_out[pl.ds(b, 1), :]
        cast_out[d, 14:16, :] = jnp.zeros((2, LANES), F32)


def moments_call(pos, mass, fill, cells, sends, placing):
    bins, doms = mass.shape[0], cells.shape[1]
    return pl.pallas_call(
        moments_kernel,
        out_shape=(
            pltpu.VMEM((bins, WIDTH), BF16),
            pltpu.VMEM((bins, LANES), F32),
            pltpu.VMEM((doms, 16, LANES), F32),
        ),
        in_specs=[VMEM] * 4 + [SMEM, VMEM],
        out_specs=(VMEM,) * 3,
        scratch_shapes=[
            pltpu.VMEM((SLOTS, 8, LANES), F32),
            pltpu.VMEM((4, LANES, LANES), F32),
        ],
        cost_estimate=pl.CostEstimate(flops=6_000_000, bytes_accessed=600_000, transcendentals=0),
        name="moments",
    )(pos, mass, fill, cells, sends, placing)


def stage_kernel(core, regions, pos, lists, placing, target, source, offset, fill, sends, after, *rest):
    ins = (pos, lists, placing, target, source, offset, fill, sends)
    outs, token, arrived = rest[: len(ins)], rest[-2], rest[-1]
    copies = [pltpu.make_async_copy(a, b, arrived.at[n]) for n, (a, b) in enumerate(zip(ins, outs))]
    for copy in copies:
        copy.start()
    token[...] = after[0:8, :]
    for copy in copies:
        copy.wait()
    ids = outs[1][...]
    doms = sends.shape[1]
    half = regions // 2 * doms
    tops = 2 * half
    region = lax.div(ids, doms)
    cell = ids - tops
    outs[1][...] = jnp.where(
        ids < tops,
        ((region & 1) ^ core[0]) * half + lax.div(region, 2) * doms + lax.rem(ids, doms),
        jnp.where(cell < doms * SENT, tops + lax.rem(cell, SENT) * doms + lax.div(cell, SENT), ids),
    )


def stage_call(core, regions, after, *arrays):
    def kernel(core_ref, *refs):
        stage_kernel(core_ref, regions, *refs)

    return pl.pallas_call(
        kernel,
        out_shape=tuple(pltpu.VMEM(a.shape, a.dtype) for a in arrays) + (pltpu.VMEM((8, LANES), F32),),
        in_specs=[SMEM] + [HBM] * len(arrays) + [VMEM],
        out_specs=(VMEM,) * (len(arrays) + 1),
        scratch_shapes=[pltpu.SemaphoreType.DMA((len(arrays),))],
        compiler_params=pltpu.CompilerParams(vmem_limit_bytes=4 * 2**20),
        cost_estimate=pl.CostEstimate(flops=0, bytes_accessed=1_000_000, transcendentals=0),
        name="stage",
    )(core, *arrays, after)


def spread_kernel(got, after, out, token):
    token[...] = after[0:8, :]
    both = jnp.concatenate([got[:, 12, :], got[:, 13, :]], axis=1).astype(BF16)
    for z in range(out.shape[0]):
        out[z] = both


def spread_call(got, after, layers):
    return pl.pallas_call(
        spread_kernel,
        out_shape=(pltpu.VMEM((layers, got.shape[0], WIDTH), BF16), pltpu.VMEM((8, LANES), F32)),
        in_specs=[VMEM, VMEM],
        out_specs=(VMEM, VMEM),
        compiler_params=pltpu.CompilerParams(vmem_limit_bytes=4 * 2**20),
        cost_estimate=pl.CostEstimate(flops=0, bytes_accessed=600_000, transcendentals=0),
        name="spread",
    )(got, after)


def near_kernel(pos, live_mass, got, target, source, offset, after, near_out, back_out, rows, wide, acc):
    own = live_mass.shape[0]
    total = rows.shape[0]
    for c in range(3):
        rows[:own, c, :] = pos[c]
    rows[:own, 3, :] = live_mass[...]
    rows[own:, 0:4, :] = got[:, 0:4, :]
    rows[:, 4:, :] = jnp.zeros((total, 4, LANES), F32)
    acc[...] = jnp.zeros_like(acc)
    part = lax.broadcasted_iota(jnp.int32, (32, 4 * LANES), 0)
    lane = lax.broadcasted_iota(jnp.int32, (32, 4 * LANES), 1)
    repeat = jnp.logical_and((part & 7) == lax.div(lane, LANES), part < 24).astype(F32).astype(BF16)

    def turn(b, carry):
        value = rows[b]
        high = value.astype(BF16)
        rest = value - high.astype(F32)
        middle = rest.astype(BF16)
        low = rest - middle.astype(F32)
        parts = jnp.concatenate(
            [high.astype(F32), middle.astype(F32), low, jnp.zeros_like(value)], axis=0
        ).astype(BF16)
        wide[b] = lax.dot_general(
            parts, repeat, (((0,), (0,)), ((), ())), preferred_element_type=F32
        )
        return carry

    lax.fori_loop(0, total, turn, 0, unroll=32)

    def task(t, carry):
        i, j, o = target[0, t], source[0, t], offset[0, t]
        sx = 2.0 * (lax.div(o, 9) - 1).astype(F32)
        sy = 2.0 * (lax.rem(lax.div(o, 3), 3) - 1).astype(F32)
        sz = 2.0 * (lax.rem(o, 3) - 1).astype(F32)
        tx = rows[i, 0:1, :] - sx
        ty = rows[i, 1:2, :] - sy
        tz = rows[i, 2:3, :] - sz
        parts = []
        for n in range(LANES // 8):
            q = slice(8 * n, 8 * n + 8)
            dx = wide[j, q, :LANES] - tx
            dy = wide[j, q, LANES : 2 * LANES] - ty
            dz = wide[j, q, 2 * LANES : 3 * LANES] - tz
            d = (dx * dx + SOFTENING) + dy * dy + dz * dz
            parts.append(wide[j, q, 3 * LANES :] * lax.rsqrt(d))
        while len(parts) > 1:
            parts = [a + b for a, b in zip(parts[::2], parts[1::2])]
        same = jnp.logical_and(i == j, o == 13).astype(F32)
        own_term = (same * 0.125) * (rows[i, 3:4, :] * lax.rsqrt(jnp.full((1, LANES), SOFTENING, F32)))
        acc[i] += parts[0] - own_term
        return carry

    lax.fori_loop(0, target.shape[1], task, 0, unroll=8)
    near = jnp.sum(acc[...], axis=1)
    near_out[...] = near[:own]
    back_out[...] = near[own:]


def near_call(pos, live_mass, got, target, source, offset, after):
    own = live_mass.shape[0]
    total = own + got.shape[0]
    return pl.pallas_call(
        near_kernel,
        out_shape=(pltpu.VMEM((own, LANES), F32), pltpu.VMEM((total - own, LANES), F32)),
        in_specs=[VMEM, VMEM, VMEM, SMEM, SMEM, SMEM, VMEM],
        out_specs=(VMEM, VMEM),
        cost_estimate=pl.CostEstimate(flops=26_000_000, bytes_accessed=600_000, transcendentals=2_000_000),
        scratch_shapes=[
            pltpu.VMEM((total, 8, LANES), F32),
            pltpu.VMEM((total, LANES, 4 * LANES), F32),
            pltpu.VMEM((total, 8, LANES), F32),
        ],
        compiler_params=pltpu.CompilerParams(vmem_limit_bytes=20 * 2**20),
        name="near",
    )(pos, live_mass, got, target, source, offset, after)


def far_kernel(mine, other, got, leaf, lists, ops, placing, pos, out, table, far_cols, local_rows, flat, held, arrived):
    bins = lists.shape[0]
    entries = lists.shape[1]
    coeffs = ops.shape[0]
    span = ops.shape[1] // PIECES
    copies = [
        pltpu.make_async_copy(
            ops.at[:, span * n : span * (n + 1)], held.at[:, span * n : span * (n + 1)], arrived.at[n]
        )
        for n in range(PIECES)
    ]
    for copy in copies:
        copy.start()
    half = mine.shape[0]
    tops = 2 * half
    doms = got.shape[0]
    sent = SENT
    table[:half] = mine[...]
    table[half:tops] = other[...]
    for s in range(sent):
        table[tops + doms * s : tops + doms * (s + 1), :LANES] = got[:, 4 + 2 * s, :].astype(BF16)
        table[tops + doms * s : tops + doms * (s + 1), LANES:] = got[:, 5 + 2 * s, :].astype(BF16)
    used = tops + doms * sent
    table[used : used + bins] = leaf[...]
    used += bins
    table[used:] = jnp.zeros((table.shape[0] - used, WIDTH), BF16)
    ids = lists[...]
    rows = lax.broadcasted_iota(jnp.int32, (bins, table.shape[0]), 1)
    lane = lax.broadcasted_iota(jnp.int32, (bins, LANES), 1)
    local = None
    carry = None
    done = 0
    for n in range(0, entries, 8):
        pick = jnp.concatenate(
            [(ids[:, k : k + 1] == rows).astype(F32).astype(BF16) for k in range(n, n + 8)], axis=0
        )
        picked = jnp.dot(pick, table[...], preferred_element_type=F32)
        for k in range(n, n + 8):
            one = picked[bins * (k - n) : bins * (k - n + 1)]
            tile, shift = divmod(k * coeffs, LANES)
            first, second = one[:, :LANES], one[:, LANES:]
            if shift:
                first, second = pltpu.roll(first, shift, 1), pltpu.roll(second, shift, 1)
                before = lane < shift
                start = jnp.where(before, carry, first)
                middle = jnp.where(before, first, second)
                end = jnp.where(before, second, 0.0)
            else:
                start, middle, end = first, second, None
            flat[:, LANES * tile : LANES * (tile + 1)] = start.astype(BF16)
            if shift + coeffs >= 2 * LANES:
                flat[:, LANES * (tile + 1) : LANES * (tile + 2)] = middle.astype(BF16)
                carry = end
            else:
                carry = middle
        ready = (n + 8) * coeffs // LANES * LANES
        while done < PIECES and span * (done + 1) <= ready:
            columns = slice(span * done, span * (done + 1))
            copies[done].wait()
            term = lax.dot_general(
                flat[:, columns], held[:, columns], (((1,), (1,)), ((), ())), preferred_element_type=F32
            )
            local = term if local is None else local + term
            done += 1
    local = jnp.concatenate([local, jnp.zeros((bins, WIDTH - coeffs), F32)], axis=1)
    spread = None
    rest = local
    for _ in range(3):
        piece = rest.astype(BF16)
        rest = rest - piece.astype(F32)
        term = lax.dot_general(placing[...], piece, (((1,), (1,)), ((), ())), preferred_element_type=F32)
        spread = term if spread is None else spread + term
    local_rows[...] = jnp.concatenate([spread[SLOTS * j : SLOTS * (j + 1)] for j in range(4)], axis=1)
    lane_group = lax.div(lax.broadcasted_iota(jnp.int32, (8, LANES), 1), bins)
    wide = far_cols
    for c in range(3):
        wide[c] = four_wide(pos[c])

    def step(i, carry):
        series = []
        for half in range(2):
            at = pl.ds(pl.multiple_of(16 * i + 8 * half, 8), 8)
            tx = chebyshev(wide[0, at, :])
            ty = chebyshev(wide[1, at, :])
            tz = grouped(chebyshev(wide[2, at, :]), lane_group)
            series.append((at, tx, ty, tz))
        totals = [None, None]
        g = 0
        while g < len(GROUPS):
            ax, ay, _ = GROUPS[g]
            inner = [None, None]
            while g < len(GROUPS) and GROUPS[g][:2] == (ax, ay):
                row = local_rows[g : g + 1, :]
                for h in range(2):
                    value = series[h][3][GROUPS[g][2]] * row
                    inner[h] = value if inner[h] is None else inner[h] + value
                g += 1
            for h in range(2):
                _, tx, ty, _ = series[h]
                value = inner[h]
                if ax:
                    value = value * tx[ax]
                if ay:
                    value = value * ty[ay]
                totals[h] = value if totals[h] is None else totals[h] + value
        for h in range(2):
            wide[3, series[h][0], :] = totals[h]
        return carry

    lax.fori_loop(0, 8, step, 0)
    spread_far = wide[3].T
    far = spread_far[:bins]
    for j in range(1, 4):
        far = far + spread_far[bins * j : bins * (j + 1)]
    out[...] = far


def far_call(mine, other, got, leaf, lists, ops, placing, pos):
    bins = lists.shape[0]
    table_rows = -(-(2 * mine.shape[0] + 4 * got.shape[0] + bins) // 256) * 256
    return pl.pallas_call(
        far_kernel,
        out_shape=pltpu.VMEM((bins, LANES), F32),
        in_specs=[VMEM] * 5 + [HBM] + [VMEM] * 2,
        out_specs=VMEM,
        scratch_shapes=[
            pltpu.VMEM((table_rows, WIDTH), BF16),
            pltpu.VMEM((4, LANES, LANES), F32),
            pltpu.VMEM((SLOTS, LANES), F32),
            pltpu.VMEM((bins, ops.shape[1]), BF16),
            pltpu.VMEM(ops.shape, BF16),
            pltpu.SemaphoreType.DMA((PIECES,)),
        ],
        compiler_params=pltpu.CompilerParams(vmem_limit_bytes=16 * 2**20),
        cost_estimate=pl.CostEstimate(flops=5_000_000_000, bytes_accessed=12_000_000, transcendentals=0),
        name="far",
    )(mine, other, got, leaf, lists, ops, placing, pos)


def combine_kernel(far, near, back, fill, sends, out, homes):
    homes[...] = far[...] + near[...]
    for d in range(back.shape[0]):
        homes[pl.ds(sends[0, d], 1), :] += back[d : d + 1, :]
    out[...] = jnp.where(live_rows(fill[...], homes), homes[...], 0.0)


def combine_call(far, near, back, fill, sends):
    return pl.pallas_call(
        combine_kernel,
        out_shape=jax.ShapeDtypeStruct(far.shape, F32),
        in_specs=[VMEM] * 4 + [SMEM],
        out_specs=VMEM,
        scratch_shapes=[pltpu.VMEM(far.shape, F32)],
        compiler_params=pltpu.CompilerParams(vmem_limit_bytes=4 * 2**20),
        name="combine",
    )(far, near, back, fill, sends)


def shards(positions, masses, fill, translations, m2l_lists, cell_sends, bin_sends, task_target, task_source, task_offset):
    pos = jnp.transpose(positions[0, 0], (1, 0, 2))
    mass = masses[0, 0]
    fill_row = fill[0]
    cells = cell_sends[0, 0].T
    sends = bin_sends.reshape(1, -1)
    placing = jnp.asarray(placing_matrix(), BF16)
    doms = cells.shape[1]
    layers = lax.axis_size("z")
    core = lax.axis_index("core").astype(jnp.int32).reshape(1)
    leaf, live_mass, cast = moments_call(pos, mass, fill_row, cells, sends, placing)
    got = lax.all_to_all(cast, "dom", split_axis=0, concat_axis=0, tiled=True)
    pos, ids, placing, target, source, offset, fill_row, sends, staged = stage_call(
        core, layers * lax.axis_size("core"), live_mass,
        pos, m2l_lists[0, 0], placing, task_target[0], task_source[0], task_offset[0], fill_row, sends,
    )
    layered, ready = spread_call(got, staged, layers)
    column = lax.all_to_all(layered, "z", split_axis=0, concat_axis=0, tiled=True)
    near, back = near_call(pos, live_mass, got, target, source, offset, ready)
    column, near, back = lax.optimization_barrier((column, near, back))
    returned = lax.all_to_all(back.reshape(doms, 1, LANES), "dom", split_axis=0, concat_axis=0, tiled=True)
    mine = column.reshape(-1, WIDTH)
    other = lax.ppermute(mine, "core", [(0, 1), (1, 0)])
    far = far_call(mine, other, got, leaf, ids, pltpu.with_memory_space_constraint(translations, pltpu.HBM), placing, pos)
    out = combine_call(far, near, returned.reshape(doms, LANES), fill_row, sends)
    return out[None, None]


def solution(mesh):
    regions, doms = mesh.devices.shape
    cores = 2
    split = jax.sharding.Mesh(mesh.devices.reshape(regions // cores, cores, doms), ("z", "core", "dom"))

    def at(*rest):
        return P(("z", "core"), "dom", *rest)

    return jax.shard_map(
        shards,
        mesh=split,
        in_specs=(at(), at(), at(), P(), at(), at(), at(), at(), at(), at()),
        out_specs=at(),
        check_vma=False,
    )
```

```python
import functools
import jax
import jax.numpy as jnp
import numpy as np
from jax import lax
from jax.experimental import pallas as pl
from jax.experimental.pallas import tpu as pltpu
from jax.sharding import PartitionSpec as P

ORDER = 8
SOFTENING = 0.01
LANES = 128
WIDTH = 256
PIECES = 5
SENT = 4
END = 40
SLOTS = 64
F32 = jnp.float32
BF16 = jnp.bfloat16
VMEM = pl.BlockSpec(memory_space=pltpu.VMEM)
HBM = pl.BlockSpec(memory_space=pltpu.HBM)
SMEM = pl.BlockSpec(memory_space=pltpu.SMEM)


def coefficient_groups():
    groups = []
    for ax in range(ORDER + 1):
        for ay in range(ORDER + 1 - ax):
            for part in range((ORDER - ax - ay) // 4 + 1):
                groups.append((ax, ay, part))
    return groups


GROUPS = coefficient_groups()


def placing_matrix():
    index, at = {}, 0
    for total in range(ORDER + 1):
        for ax in range(total, -1, -1):
            for ay in range(total - ax, -1, -1):
                index[(ax, ay, total - ax - ay)] = at
                at += 1
    placing = np.zeros((WIDTH, WIDTH), np.float32)
    for row, (ax, ay, part) in enumerate(GROUPS):
        for j in range(4):
            place = index.get((ax, ay, 4 * part + j))
            if place is not None:
                placing[j * SLOTS + row, place] = 1.0
    return placing


def chebyshev(t):
    series = [jnp.ones_like(t), t]
    for _ in range(2, ORDER + 1):
        series.append(2.0 * t * series[-1] - series[-2])
    return series


def grouped(series, lane_group):
    parts = []
    for n in range(3):
        value = series[4 * n]
        for j in range(1, 4):
            other = series[4 * n + j] if 4 * n + j <= ORDER else jnp.zeros_like(value)
            value = jnp.where(lane_group == j, other, value)
        parts.append(value)
    return parts


def four_wide(rows):
    return jnp.concatenate([rows] * 4, axis=0).T


def live_rows(fill_row, masses):
    bins, slots = masses.shape
    eye = lax.broadcasted_iota(jnp.int32, (bins, bins), 0) == lax.broadcasted_iota(
        jnp.int32, (bins, bins), 1
    )
    fill_col = jnp.sum(
        jnp.where(eye, fill_row.astype(F32), 0.0), axis=1, keepdims=True
    )
    slot = lax.broadcasted_iota(jnp.int32, (bins, slots), 1).astype(F32)
    return slot < fill_col


def moments_kernel(pos, mass, fill, cells, sends, placing, leaf_out, live_out, wide, cast_out, acc, rows):
    bins = mass.shape[0]
    live_mass = jnp.where(live_rows(fill[...], mass[...]), mass[...], 0.0)
    live_out[...] = live_mass
    for c in range(3):
        wide[c] = four_wide(pos[c])
    wide[3] = four_wide(live_mass)
    acc[...] = jnp.zeros_like(acc)
    lane_group = lax.div(lax.broadcasted_iota(jnp.int32, (8, LANES), 1), bins)

    def step(i, carry):
        sums = [None] * len(GROUPS)
        for half in range(2):
            at = pl.ds(pl.multiple_of(16 * i + 8 * half, 8), 8)
            tx = chebyshev(wide[0, at, :])
            ty = chebyshev(wide[1, at, :])
            m = wide[3, at, :]
            tz = [v * m for v in grouped(chebyshev(wide[2, at, :]), lane_group)]
            last = None
            for g, (ax, ay, part) in enumerate(GROUPS):
                if last is None or last[0] != (ax, ay):
                    last = ((ax, ay), tx[ax] * ty[ay] if ax and ay else (tx[ax] if ax else ty[ay]))
                value = last[1] * tz[part] if (ax or ay) else tz[part]
                sums[g] = value if sums[g] is None else sums[g] + value
        for g in range(len(GROUPS)):
            acc[g] += sums[g]
        return carry

    lax.fori_loop(0, 8, step, 0)
    raw = jnp.sum(acc[...], axis=1).T
    moments = jnp.concatenate([raw[bins * j : bins * (j + 1)] for j in range(4)], axis=1)
    top = jnp.sum(moments, axis=0, keepdims=True) * (1.0 / bins)
    both = jnp.concatenate([moments, jnp.broadcast_to(top, (cells.shape[1], WIDTH))], axis=0).astype(BF16)
    placed = jnp.dot(both, placing[...], preferred_element_type=F32)
    leaf = placed[:bins].astype(BF16)
    leaf_out[...] = leaf
    doms = cells.shape[1]
    rows[:, 12, :] = placed[bins:, :LANES]
    ends = [placed[bins:, LANES:]]
    for s in range(SENT):
        pick = (lax.broadcasted_iota(jnp.int32, (bins, doms), 0) == cells[s : s + 1, :]).astype(F32).astype(BF16)
        one = lax.dot_general(pick, leaf, (((0,), (0,)), ((), ())), preferred_element_type=F32)
        rows[:, 8 + s, :] = one[:, :LANES]
        ends.append(one[:, LANES:])
    rows[:, 13, :] = ends[1] + pltpu.roll(ends[2], END, 1) + pltpu.roll(ends[3], 2 * END, 1)
    rows[:, 14, :] = ends[4] + pltpu.roll(ends[0], END, 1)
    rows[:, 15, :] = jnp.zeros((doms, LANES), F32)
    for d in range(doms):
        b = sends[0, d]
        for c in range(3):
            rows[d, c : c + 1, :] = pos[c, pl.ds(b, 1), :]
        rows[d, 3:4, :] = live_out[pl.ds(b, 1), :]
    value = rows[:, 0:4, :]
    rows[:, 4:8, :] = value - value.astype(BF16).astype(F32)
    cast_out[...] = rows[...].astype(BF16)


def moments_call(pos, mass, fill, cells, sends, placing):
    bins, doms = mass.shape[0], cells.shape[1]
    return pl.pallas_call(
        moments_kernel,
        out_shape=(
            pltpu.VMEM((bins, WIDTH), BF16),
            pltpu.VMEM((bins, LANES), F32),
            pltpu.VMEM((4, LANES, LANES), F32),
            pltpu.VMEM((doms, 16, LANES), BF16),
        ),
        in_specs=[VMEM] * 4 + [SMEM, VMEM],
        out_specs=(VMEM,) * 4,
        scratch_shapes=[
            pltpu.VMEM((SLOTS, 8, LANES), F32),
            pltpu.VMEM((doms, 16, LANES), F32),
        ],
        cost_estimate=pl.CostEstimate(flops=6_000_000, bytes_accessed=600_000, transcendentals=0),
        name="moments",
    )(pos, mass, fill, cells, sends, placing)


def stage_kernel(core, regions, pos, lists, placing, target, source, offset, fill, sends, after, *rest):
    ins = (pos, lists, placing, target, source, offset, fill, sends)
    outs, token, arrived = rest[: len(ins)], rest[-2], rest[-1]
    copies = [pltpu.make_async_copy(a, b, arrived.at[n]) for n, (a, b) in enumerate(zip(ins, outs))]
    for copy in copies:
        copy.start()
    token[...] = after[0:8, :]
    for copy in copies:
        copy.wait()
    ids = outs[1][...]
    doms = sends.shape[1]
    half = regions // 2 * doms
    tops = 2 * half
    region = lax.div(ids, doms)
    cell = ids - tops
    outs[1][...] = jnp.where(
        ids < tops,
        ((region & 1) ^ core[0]) * half + lax.div(region, 2) * doms + lax.rem(ids, doms),
        jnp.where(cell < doms * SENT, tops + lax.rem(cell, SENT) * doms + lax.div(cell, SENT), ids),
    )


def stage_call(core, regions, after, *arrays):
    def kernel(core_ref, *refs):
        stage_kernel(core_ref, regions, *refs)

    return pl.pallas_call(
        kernel,
        out_shape=tuple(pltpu.VMEM(a.shape, a.dtype) for a in arrays) + (pltpu.VMEM((8, LANES), F32),),
        in_specs=[SMEM] + [HBM] * len(arrays) + [VMEM],
        out_specs=(VMEM,) * (len(arrays) + 1),
        scratch_shapes=[pltpu.SemaphoreType.DMA((len(arrays),))],
        compiler_params=pltpu.CompilerParams(vmem_limit_bytes=4 * 2**20),
        cost_estimate=pl.CostEstimate(flops=0, bytes_accessed=1_000_000, transcendentals=0),
        name="stage",
    )(core, *[pltpu.with_memory_space_constraint(a, pltpu.HBM) for a in arrays], after)


def spread_kernel(got, after, out, token, rows):
    token[...] = after[...]
    rows[...] = got[...].astype(F32)
    doms = got.shape[0]
    half = doms // 2
    first = rows[:, 12, :].astype(BF16)
    end = pltpu.roll(rows[:, 14, :], LANES - END, 1)
    lane = lax.broadcasted_iota(jnp.int32, (half, LANES), 1)
    ends = jnp.where(lane < LANES // 2, end[:half], pltpu.roll(end[half:], LANES // 2, 1)).astype(BF16)
    for z in range(out.shape[0]):
        out[z, :doms, :] = first
        out[z, doms:, :] = ends


def spread_call(got, after, layers):
    return pl.pallas_call(
        spread_kernel,
        out_shape=(pltpu.VMEM((layers, got.shape[0] * 3 // 2, LANES), BF16), pltpu.VMEM((8, LANES), F32)),
        in_specs=[VMEM, VMEM],
        out_specs=(VMEM, VMEM),
        scratch_shapes=[pltpu.VMEM(got.shape, F32)],
        compiler_params=pltpu.CompilerParams(vmem_limit_bytes=4 * 2**20),
        cost_estimate=pl.CostEstimate(flops=0, bytes_accessed=600_000, transcendentals=0),
        name="spread",
    )(got, after)


def near_kernel(pos, live_mass, got, target, source, offset, after, near_out, back_out, rows, wide, acc):
    own = live_mass.shape[0]
    total = rows.shape[0]
    for c in range(3):
        rows[:own, c, :] = pos[c]
    rows[:own, 3, :] = live_mass[...]
    arrived = got[...].astype(F32)
    rows[own:, 0:4, :] = arrived[:, 0:4, :] + arrived[:, 4:8, :]
    rows[:, 4:, :] = jnp.zeros((total, 4, LANES), F32)
    acc[...] = jnp.zeros_like(acc)
    part = lax.broadcasted_iota(jnp.int32, (32, 4 * LANES), 0)
    lane = lax.broadcasted_iota(jnp.int32, (32, 4 * LANES), 1)
    repeat = jnp.logical_and((part & 7) == lax.div(lane, LANES), part < 24).astype(F32).astype(BF16)

    def turn(b, carry):
        value = rows[b]
        high = value.astype(BF16)
        rest = value - high.astype(F32)
        middle = rest.astype(BF16)
        low = rest - middle.astype(F32)
        parts = jnp.concatenate(
            [high.astype(F32), middle.astype(F32), low, jnp.zeros_like(value)], axis=0
        ).astype(BF16)
        wide[b] = lax.dot_general(
            parts, repeat, (((0,), (0,)), ((), ())), preferred_element_type=F32
        )
        return carry

    lax.fori_loop(0, total, turn, 0, unroll=32)

    def task(t, carry):
        i, j, o = target[0, t], source[0, t], offset[0, t]
        sx = 2.0 * (lax.div(o, 9) - 1).astype(F32)
        sy = 2.0 * (lax.rem(lax.div(o, 3), 3) - 1).astype(F32)
        sz = 2.0 * (lax.rem(o, 3) - 1).astype(F32)
        tx = rows[i, 0:1, :] - sx
        ty = rows[i, 1:2, :] - sy
        tz = rows[i, 2:3, :] - sz
        parts = []
        for n in range(LANES // 8):
            q = slice(8 * n, 8 * n + 8)
            dx = wide[j, q, :LANES] - tx
            dy = wide[j, q, LANES : 2 * LANES] - ty
            dz = wide[j, q, 2 * LANES : 3 * LANES] - tz
            d = (dx * dx + SOFTENING) + dy * dy + dz * dz
            parts.append(wide[j, q, 3 * LANES :] * lax.rsqrt(d))
        while len(parts) > 1:
            parts = [a + b for a, b in zip(parts[::2], parts[1::2])]
        same = jnp.logical_and(i == j, o == 13).astype(F32)
        own_term = (same * 0.125) * (rows[i, 3:4, :] * lax.rsqrt(jnp.full((1, LANES), SOFTENING, F32)))
        acc[i] += parts[0] - own_term
        return carry

    lax.fori_loop(0, target.shape[1], task, 0, unroll=8)
    near = jnp.sum(acc[...], axis=1)
    near_out[...] = near[:own]
    back_out[...] = near[own:]


def near_call(pos, live_mass, got, target, source, offset, after):
    own = live_mass.shape[0]
    total = own + got.shape[0]
    return pl.pallas_call(
        near_kernel,
        out_shape=(pltpu.VMEM((own, LANES), F32), pltpu.VMEM((total - own, LANES), F32)),
        in_specs=[VMEM, VMEM, VMEM, SMEM, SMEM, SMEM, VMEM],
        out_specs=(VMEM, VMEM),
        cost_estimate=pl.CostEstimate(flops=26_000_000, bytes_accessed=600_000, transcendentals=2_000_000),
        scratch_shapes=[
            pltpu.VMEM((total, 8, LANES), F32),
            pltpu.VMEM((total, LANES, 4 * LANES), F32),
            pltpu.VMEM((total, 8, LANES), F32),
        ],
        compiler_params=pltpu.CompilerParams(vmem_limit_bytes=20 * 2**20),
        name="near",
    )(pos, live_mass, got, target, source, offset, after)


def picked_rows(ids, first, table, n, count):
    rows = lax.broadcasted_iota(jnp.int32, (ids.shape[0], table.shape[0]), 1) + first
    pick = jnp.concatenate(
        [(ids[:, k : k + 1] == rows).astype(F32).astype(BF16) for k in range(n, n + count)], axis=0
    )
    return jnp.dot(pick, table[...], preferred_element_type=F32)


def lay_out(picked, n, count, coeffs, carry, store):
    bins = picked.shape[0] // count
    lane = lax.broadcasted_iota(jnp.int32, (bins, LANES), 1)
    for k in range(n, n + count):
        one = picked[bins * (k - n) : bins * (k - n + 1)]
        tile, shift = divmod(k * coeffs, LANES)
        first, second = one[:, :LANES], one[:, LANES:]
        if shift:
            first, second = pltpu.roll(first, shift, 1), pltpu.roll(second, shift, 1)
            before = lane < shift
            start = jnp.where(before, carry, first)
            middle = jnp.where(before, first, second)
            end = jnp.where(before, second, 0.0)
        else:
            start, middle, end = first, second, None
        store(tile, start)
        if shift + coeffs >= 2 * LANES:
            store(tile + 1, middle)
            carry = end
        else:
            carry = middle
    return carry


def rest_kernel(tops, coeffs, got, leaf, lists, rest_out, rows, table):
    doms = got.shape[0]
    bins, entries = lists.shape
    rows[...] = got[...].astype(F32)
    for s in range(SENT):
        table[doms * s : doms * (s + 1), :LANES] = rows[:, 8 + s, :].astype(BF16)
        end = rows[:, 14, :] if s == 3 else rows[:, 13, :]
        if 0 < s < 3:
            end = pltpu.roll(end, LANES - s * END, 1)
        table[doms * s : doms * (s + 1), LANES:] = end.astype(BF16)
    used = doms * SENT
    table[used : used + bins] = leaf[...]
    used += bins
    table[used:] = jnp.zeros((table.shape[0] - used, WIDTH), BF16)
    ids = lists[...]

    def store(tile, value):
        rest_out[:, LANES * tile : LANES * (tile + 1)] = value.astype(BF16)

    carry = None
    for n in range(0, entries, 8):
        carry = lay_out(picked_rows(ids, tops, table, n, 8), n, 8, coeffs, carry, store)


def rest_call(tops, coeffs, got, leaf, lists):
    bins, entries = lists.shape
    table_rows = -(-(SENT * got.shape[0] + bins) // 256) * 256
    return pl.pallas_call(
        functools.partial(rest_kernel, tops, coeffs),
        out_shape=pltpu.VMEM((bins, entries * coeffs), BF16),
        in_specs=[VMEM] * 3,
        out_specs=VMEM,
        scratch_shapes=[pltpu.VMEM(got.shape, F32), pltpu.VMEM((table_rows, WIDTH), BF16)],
        compiler_params=pltpu.CompilerParams(vmem_limit_bytes=8 * 2**20),
        cost_estimate=pl.CostEstimate(flops=1_000_000_000, bytes_accessed=2_000_000, transcendentals=0),
        name="rest",
    )(got, leaf, lists)


def far_kernel(mine, other, rest, lists, ops, placing, wide, out, table, far_cols, local_rows, flat, held, arrived):
    bins, entries = lists.shape
    coeffs = ops.shape[0]
    span = ops.shape[1] // PIECES
    copies = [
        pltpu.make_async_copy(
            ops.at[:, span * n : span * (n + 1)], held.at[:, span * n : span * (n + 1)], arrived.at[n]
        )
        for n in range(PIECES)
    ]
    for copy in copies:
        copy.start()
    layers, doms = mine.shape[0], mine.shape[1] * 2 // 3
    half = doms // 2
    for z in range(2 * layers):
        from_core, layer = (mine, z) if z < layers else (other, z - layers)
        table[doms * z : doms * (z + 1), :LANES] = from_core[layer, :doms, :]
        ends = from_core[layer, doms:, :]
        table[doms * z : doms * z + half, LANES:] = ends
        table[doms * z + half : doms * (z + 1), LANES:] = pltpu.roll(ends.astype(F32), LANES // 2, 1).astype(BF16)
    ids = lists[...]

    def store(tile, value):
        columns = slice(LANES * tile, LANES * (tile + 1))
        flat[:, columns] = (value + rest[:, columns].astype(F32)).astype(BF16)

    local = None
    carry = None
    done = 0
    for n in range(0, entries, 8):
        carry = lay_out(picked_rows(ids, 0, table, n, 8), n, 8, coeffs, carry, store)
        ready = (n + 8) * coeffs // LANES * LANES
        while done < PIECES and span * (done + 1) <= ready:
            columns = slice(span * done, span * (done + 1))
            copies[done].wait()
            term = lax.dot_general(
                flat[:, columns], held[:, columns], (((1,), (1,)), ((), ())), preferred_element_type=F32
            )
            local = term if local is None else local + term
            done += 1
    local = jnp.concatenate([local, jnp.zeros((bins, WIDTH - coeffs), F32)], axis=1)
    spread = None
    rest = local
    for _ in range(3):
        piece = rest.astype(BF16)
        rest = rest - piece.astype(F32)
        term = lax.dot_general(placing[...], piece, (((1,), (1,)), ((), ())), preferred_element_type=F32)
        spread = term if spread is None else spread + term
    local_rows[...] = jnp.concatenate([spread[SLOTS * j : SLOTS * (j + 1)] for j in range(4)], axis=1)
    lane_group = lax.div(lax.broadcasted_iota(jnp.int32, (8, LANES), 1), bins)

    def step(i, carry):
        series = []
        for half in range(2):
            at = pl.ds(pl.multiple_of(16 * i + 8 * half, 8), 8)
            tx = chebyshev(wide[0, at, :])
            ty = chebyshev(wide[1, at, :])
            tz = grouped(chebyshev(wide[2, at, :]), lane_group)
            series.append((at, tx, ty, tz))
        totals = [None, None]
        g = 0
        while g < len(GROUPS):
            ax, ay, _ = GROUPS[g]
            inner = [None, None]
            while g < len(GROUPS) and GROUPS[g][:2] == (ax, ay):
                row = local_rows[g : g + 1, :]
                for h in range(2):
                    value = series[h][3][GROUPS[g][2]] * row
                    inner[h] = value if inner[h] is None else inner[h] + value
                g += 1
            for h in range(2):
                _, tx, ty, _ = series[h]
                value = inner[h]
                if ax:
                    value = value * tx[ax]
                if ay:
                    value = value * ty[ay]
                totals[h] = value if totals[h] is None else totals[h] + value
        for h in range(2):
            far_cols[series[h][0], :] = totals[h]
        return carry

    lax.fori_loop(0, 8, step, 0)
    spread_far = far_cols[...].T
    far = spread_far[:bins]
    for j in range(1, 4):
        far = far + spread_far[bins * j : bins * (j + 1)]
    out[...] = far


def far_call(mine, other, rest, lists, ops, placing, wide):
    bins = lists.shape[0]
    table_rows = 2 * mine.shape[0] * mine.shape[1] * 2 // 3
    return pl.pallas_call(
        far_kernel,
        out_shape=pltpu.VMEM((bins, LANES), F32),
        in_specs=[VMEM] * 4 + [HBM] + [VMEM] * 2,
        out_specs=VMEM,
        scratch_shapes=[
            pltpu.VMEM((table_rows, WIDTH), BF16),
            pltpu.VMEM((LANES, LANES), F32),
            pltpu.VMEM((SLOTS, LANES), F32),
            pltpu.VMEM((bins, ops.shape[1]), BF16),
            pltpu.VMEM(ops.shape, BF16),
            pltpu.SemaphoreType.DMA((PIECES,)),
        ],
        compiler_params=pltpu.CompilerParams(vmem_limit_bytes=16 * 2**20),
        cost_estimate=pl.CostEstimate(flops=5_000_000_000, bytes_accessed=12_000_000, transcendentals=0),
        name="far",
    )(mine, other, rest, lists, pltpu.with_memory_space_constraint(ops, pltpu.HBM), placing, wide)


def combine_kernel(far, near, back, fill, sends, out, homes):
    homes[...] = far[...] + near[...]
    for d in range(back.shape[0]):
        homes[pl.ds(sends[0, d], 1), :] += back[d : d + 1, :]
    out[...] = jnp.where(live_rows(fill[...], homes), homes[...], 0.0)


def combine_call(far, near, back, fill, sends):
    return pl.pallas_call(
        combine_kernel,
        out_shape=jax.ShapeDtypeStruct(far.shape, F32),
        in_specs=[VMEM] * 4 + [SMEM],
        out_specs=VMEM,
        scratch_shapes=[pltpu.VMEM(far.shape, F32)],
        compiler_params=pltpu.CompilerParams(vmem_limit_bytes=4 * 2**20),
        name="combine",
    )(far, near, back, fill, sends)


def shards(positions, masses, fill, translations, m2l_lists, cell_sends, bin_sends, task_target, task_source, task_offset):
    pos = jnp.transpose(positions[0, 0], (1, 0, 2))
    mass = masses[0, 0]
    fill_row = fill[0]
    cells = cell_sends[0, 0].T
    sends = bin_sends.reshape(1, -1)
    placing = jnp.asarray(placing_matrix(), BF16)
    doms = cells.shape[1]
    layers = lax.axis_size("z")
    core = lax.axis_index("core").astype(jnp.int32).reshape(1)
    leaf, live_mass, wide, cast = moments_call(pos, mass, fill_row, cells, sends, placing)
    got = lax.all_to_all(cast, "dom", split_axis=0, concat_axis=0, tiled=True)
    pos, ids, placing, target, source, offset, fill_row, sends, staged = stage_call(
        core, layers * lax.axis_size("core"), live_mass,
        pos, m2l_lists[0, 0], placing, task_target[0], task_source[0], task_offset[0], fill_row, sends,
    )
    layered, ready = spread_call(got, staged, layers)
    column = lax.all_to_all(layered, "z", split_axis=0, concat_axis=0, tiled=True)
    near, back = near_call(pos, live_mass, got, target, source, offset, ready)
    rest = rest_call(layers * lax.axis_size("core") * doms, translations.shape[0], got, leaf, ids)
    column, near, back, rest = lax.optimization_barrier((column, near, back, rest))
    returned = lax.all_to_all(back.reshape(doms, 1, LANES), "dom", split_axis=0, concat_axis=0, tiled=True)
    other = lax.ppermute(column, "core", [(0, 1), (1, 0)])
    far = far_call(column, other, rest, ids, translations, placing, wide)
    out = combine_call(far, near, returned.reshape(doms, LANES), fill_row, sends)
    return out[None, None]


def solution(mesh):
    regions, doms = mesh.devices.shape
    cores = 2
    split = jax.sharding.Mesh(mesh.devices.reshape(regions // cores, cores, doms), ("z", "core", "dom"))

    def at(*rest):
        return P(("z", "core"), "dom", *rest)

    return jax.shard_map(
        shards,
        mesh=split,
        in_specs=(at(), at(), at(), P(), at(), at(), at(), at(), at(), at()),
        out_specs=at(),
        check_vma=False,
    )
```

```python
import functools
import jax
import jax.numpy as jnp
import numpy as np
from jax import lax
from jax.experimental import pallas as pl
from jax.experimental.pallas import tpu as pltpu
from jax.sharding import PartitionSpec as P

ORDER = 8
SOFTENING = 0.01
LANES = 128
WIDTH = 256
PIECES = 5
SENT = 4
END = 40
SLOTS = 64
F32 = jnp.float32
BF16 = jnp.bfloat16
VMEM = pl.BlockSpec(memory_space=pltpu.VMEM)
HBM = pl.BlockSpec(memory_space=pltpu.HBM)
SMEM = pl.BlockSpec(memory_space=pltpu.SMEM)


def coefficient_groups():
    groups = []
    for ax in range(ORDER + 1):
        for ay in range(ORDER + 1 - ax):
            for part in range((ORDER - ax - ay) // 4 + 1):
                groups.append((ax, ay, part))
    return groups


GROUPS = coefficient_groups()


def placing_matrix():
    index, at = {}, 0
    for total in range(ORDER + 1):
        for ax in range(total, -1, -1):
            for ay in range(total - ax, -1, -1):
                index[(ax, ay, total - ax - ay)] = at
                at += 1
    placing = np.zeros((WIDTH, WIDTH), np.float32)
    for row, (ax, ay, part) in enumerate(GROUPS):
        for j in range(4):
            place = index.get((ax, ay, 4 * part + j))
            if place is not None:
                placing[j * SLOTS + row, place] = 1.0
    return placing


def chebyshev(t):
    series = [jnp.ones_like(t), t]
    for _ in range(2, ORDER + 1):
        series.append(2.0 * t * series[-1] - series[-2])
    return series


def grouped(series, lane_group):
    parts = []
    for n in range(3):
        value = series[4 * n]
        for j in range(1, 4):
            other = series[4 * n + j] if 4 * n + j <= ORDER else jnp.zeros_like(value)
            value = jnp.where(lane_group == j, other, value)
        parts.append(value)
    return parts


def four_wide(rows):
    return jnp.concatenate([rows] * 4, axis=0).T


def live_rows(fill_row, masses):
    bins, slots = masses.shape
    eye = lax.broadcasted_iota(jnp.int32, (bins, bins), 0) == lax.broadcasted_iota(
        jnp.int32, (bins, bins), 1
    )
    fill_col = jnp.sum(
        jnp.where(eye, fill_row.astype(F32), 0.0), axis=1, keepdims=True
    )
    slot = lax.broadcasted_iota(jnp.int32, (bins, slots), 1).astype(F32)
    return slot < fill_col


def moments_kernel(pos, mass, fill, cells, sends, placing, leaf_out, live_out, wide, cast_out, acc, rows):
    bins = mass.shape[0]
    live_mass = jnp.where(live_rows(fill[...], mass[...]), mass[...], 0.0)
    live_out[...] = live_mass
    for c in range(3):
        wide[c] = four_wide(pos[c])
    wide[3] = four_wide(live_mass)
    acc[...] = jnp.zeros_like(acc)
    lane_group = lax.div(lax.broadcasted_iota(jnp.int32, (8, LANES), 1), bins)

    def step(i, carry):
        sums = [None] * len(GROUPS)
        for half in range(2):
            at = pl.ds(pl.multiple_of(16 * i + 8 * half, 8), 8)
            tx = chebyshev(wide[0, at, :])
            ty = chebyshev(wide[1, at, :])
            m = wide[3, at, :]
            tz = [v * m for v in grouped(chebyshev(wide[2, at, :]), lane_group)]
            last = None
            for g, (ax, ay, part) in enumerate(GROUPS):
                if last is None or last[0] != (ax, ay):
                    last = ((ax, ay), tx[ax] * ty[ay] if ax and ay else (tx[ax] if ax else ty[ay]))
                value = last[1] * tz[part] if (ax or ay) else tz[part]
                sums[g] = value if sums[g] is None else sums[g] + value
        for g in range(len(GROUPS)):
            acc[g] += sums[g]
        return carry

    lax.fori_loop(0, 8, step, 0)
    raw = jnp.sum(acc[...], axis=1).T
    moments = jnp.concatenate([raw[bins * j : bins * (j + 1)] for j in range(4)], axis=1)
    top = jnp.sum(moments, axis=0, keepdims=True) * (1.0 / bins)
    both = jnp.concatenate([moments, jnp.broadcast_to(top, (cells.shape[1], WIDTH))], axis=0).astype(BF16)
    placed = jnp.dot(both, placing[...], preferred_element_type=F32)
    leaf = placed[:bins].astype(BF16)
    leaf_out[...] = leaf
    doms = cells.shape[1]
    rows[:, 12, :] = placed[bins:, :LANES]
    ends = [placed[bins:, LANES:]]
    for s in range(SENT):
        pick = (lax.broadcasted_iota(jnp.int32, (bins, doms), 0) == cells[s : s + 1, :]).astype(F32).astype(BF16)
        one = lax.dot_general(pick, leaf, (((0,), (0,)), ((), ())), preferred_element_type=F32)
        rows[:, 8 + s, :] = one[:, :LANES]
        ends.append(one[:, LANES:])
    rows[:, 13, :] = ends[1] + pltpu.roll(ends[2], END, 1) + pltpu.roll(ends[3], 2 * END, 1)
    rows[:, 14, :] = ends[4] + pltpu.roll(ends[0], END, 1)
    rows[:, 15, :] = jnp.zeros((doms, LANES), F32)
    for d in range(doms):
        b = sends[0, d]
        for c in range(3):
            rows[d, c : c + 1, :] = pos[c, pl.ds(b, 1), :]
        rows[d, 3:4, :] = live_out[pl.ds(b, 1), :]
    value = rows[:, 0:4, :]
    rows[:, 4:8, :] = value - value.astype(BF16).astype(F32)
    cast_out[...] = rows[...].astype(BF16)


def moments_call(pos, mass, fill, cells, sends, placing):
    bins, doms = mass.shape[0], cells.shape[1]
    return pl.pallas_call(
        moments_kernel,
        out_shape=(
            pltpu.VMEM((bins, WIDTH), BF16),
            pltpu.VMEM((bins, LANES), F32),
            pltpu.VMEM((4, LANES, LANES), F32),
            pltpu.VMEM((doms, 16, LANES), BF16),
        ),
        in_specs=[VMEM] * 4 + [SMEM, VMEM],
        out_specs=(VMEM,) * 4,
        scratch_shapes=[
            pltpu.VMEM((SLOTS, 8, LANES), F32),
            pltpu.VMEM((doms, 16, LANES), F32),
        ],
        cost_estimate=pl.CostEstimate(flops=6_000_000, bytes_accessed=600_000, transcendentals=0),
        name="moments",
    )(pos, mass, fill, cells, sends, placing)


def stage_kernel(core, regions, pos, lists, placing, target, source, offset, sends, after, *rest):
    ins = (pos, lists, placing, target, source, offset, sends)
    outs, token, arrived = rest[: len(ins)], rest[-2], rest[-1]
    copies = [pltpu.make_async_copy(a, b, arrived.at[n]) for n, (a, b) in enumerate(zip(ins, outs))]
    for copy in copies:
        copy.start()
    token[...] = after[0:8, :]
    for copy in copies:
        copy.wait()
    ids = outs[1][...]
    doms = sends.shape[1]
    half = regions // 2 * doms
    tops = 2 * half
    region = lax.div(ids, doms)
    cell = ids - tops
    outs[1][...] = jnp.where(
        ids < tops,
        ((region & 1) ^ core[0]) * half + lax.div(region, 2) * doms + lax.rem(ids, doms),
        jnp.where(cell < doms * SENT, tops + lax.rem(cell, SENT) * doms + lax.div(cell, SENT), ids),
    )


def stage_call(core, regions, after, *arrays):
    def kernel(core_ref, *refs):
        stage_kernel(core_ref, regions, *refs)

    return pl.pallas_call(
        kernel,
        out_shape=tuple(pltpu.VMEM(a.shape, a.dtype) for a in arrays) + (pltpu.VMEM((8, LANES), F32),),
        in_specs=[SMEM] + [HBM] * len(arrays) + [VMEM],
        out_specs=(VMEM,) * (len(arrays) + 1),
        scratch_shapes=[pltpu.SemaphoreType.DMA((len(arrays),))],
        compiler_params=pltpu.CompilerParams(vmem_limit_bytes=4 * 2**20),
        cost_estimate=pl.CostEstimate(flops=0, bytes_accessed=1_000_000, transcendentals=0),
        name="stage",
    )(core, *[pltpu.with_memory_space_constraint(a, pltpu.HBM) for a in arrays], after)


def spread_kernel(got, after, out, token, rows):
    token[...] = after[...]
    rows[...] = got[...].astype(F32)
    doms = got.shape[0]
    half = doms // 2
    first = rows[:, 12, :].astype(BF16)
    end = pltpu.roll(rows[:, 14, :], LANES - END, 1)
    lane = lax.broadcasted_iota(jnp.int32, (half, LANES), 1)
    ends = jnp.where(lane < LANES // 2, end[:half], pltpu.roll(end[half:], LANES // 2, 1)).astype(BF16)
    for z in range(out.shape[0]):
        out[z, :doms, :] = first
        out[z, doms:, :] = ends


def spread_call(got, after, layers):
    return pl.pallas_call(
        spread_kernel,
        out_shape=(pltpu.VMEM((layers, got.shape[0] * 3 // 2, LANES), BF16), pltpu.VMEM((8, LANES), F32)),
        in_specs=[VMEM, VMEM],
        out_specs=(VMEM, VMEM),
        scratch_shapes=[pltpu.VMEM(got.shape, F32)],
        compiler_params=pltpu.CompilerParams(vmem_limit_bytes=4 * 2**20),
        cost_estimate=pl.CostEstimate(flops=0, bytes_accessed=600_000, transcendentals=0),
        name="spread",
    )(got, after)


def near_kernel(pos, live_mass, got, target, source, offset, after, near_out, back_out, rows, wide, acc):
    own = live_mass.shape[0]
    total = rows.shape[0]
    for c in range(3):
        rows[:own, c, :] = pos[c]
    rows[:own, 3, :] = live_mass[...]
    arrived = got[...].astype(F32)
    rows[own:, 0:4, :] = arrived[:, 0:4, :] + arrived[:, 4:8, :]
    rows[:, 4:, :] = jnp.zeros((total, 4, LANES), F32)
    acc[...] = jnp.zeros_like(acc)
    part = lax.broadcasted_iota(jnp.int32, (32, 4 * LANES), 0)
    lane = lax.broadcasted_iota(jnp.int32, (32, 4 * LANES), 1)
    repeat = jnp.logical_and((part & 7) == lax.div(lane, LANES), part < 24).astype(F32).astype(BF16)

    def turn(b, carry):
        value = rows[b]
        high = value.astype(BF16)
        rest = value - high.astype(F32)
        middle = rest.astype(BF16)
        low = rest - middle.astype(F32)
        parts = jnp.concatenate(
            [high.astype(F32), middle.astype(F32), low, jnp.zeros_like(value)], axis=0
        ).astype(BF16)
        wide[b] = lax.dot_general(
            parts, repeat, (((0,), (0,)), ((), ())), preferred_element_type=F32
        )
        return carry

    lax.fori_loop(0, total, turn, 0, unroll=32)

    def task(t, carry):
        i, j, o = target[0, t], source[0, t], offset[0, t]
        sx = 2.0 * (lax.div(o, 9) - 1).astype(F32)
        sy = 2.0 * (lax.rem(lax.div(o, 3), 3) - 1).astype(F32)
        sz = 2.0 * (lax.rem(o, 3) - 1).astype(F32)
        tx = rows[i, 0:1, :] - sx
        ty = rows[i, 1:2, :] - sy
        tz = rows[i, 2:3, :] - sz
        parts = []
        for n in range(LANES // 8):
            q = slice(8 * n, 8 * n + 8)
            dx = wide[j, q, :LANES] - tx
            dy = wide[j, q, LANES : 2 * LANES] - ty
            dz = wide[j, q, 2 * LANES : 3 * LANES] - tz
            d = (dx * dx + SOFTENING) + dy * dy + dz * dz
            parts.append(wide[j, q, 3 * LANES :] * lax.rsqrt(d))
        while len(parts) > 1:
            parts = [a + b for a, b in zip(parts[::2], parts[1::2])]
        same = jnp.logical_and(i == j, o == 13).astype(F32)
        own_term = (same * 0.125) * (rows[i, 3:4, :] * lax.rsqrt(jnp.full((1, LANES), SOFTENING, F32)))
        acc[i] += parts[0] - own_term
        return carry

    lax.fori_loop(0, target.shape[1], task, 0, unroll=8)
    near = jnp.sum(acc[...], axis=1)
    near_out[...] = near[:own]
    back_out[...] = near[own:]


def near_call(pos, live_mass, got, target, source, offset, after):
    own = live_mass.shape[0]
    total = own + got.shape[0]
    return pl.pallas_call(
        near_kernel,
        out_shape=(pltpu.VMEM((own, LANES), F32), pltpu.VMEM((total - own, LANES), F32)),
        in_specs=[VMEM, VMEM, VMEM, SMEM, SMEM, SMEM, VMEM],
        out_specs=(VMEM, VMEM),
        cost_estimate=pl.CostEstimate(flops=26_000_000, bytes_accessed=600_000, transcendentals=2_000_000),
        scratch_shapes=[
            pltpu.VMEM((total, 8, LANES), F32),
            pltpu.VMEM((total, LANES, 4 * LANES), F32),
            pltpu.VMEM((total, 8, LANES), F32),
        ],
        compiler_params=pltpu.CompilerParams(vmem_limit_bytes=20 * 2**20),
        name="near",
    )(pos, live_mass, got, target, source, offset, after)


def picked_rows(ids, first, table, n, count):
    rows = lax.broadcasted_iota(jnp.int32, (ids.shape[0], table.shape[0]), 1) + first
    pick = jnp.concatenate(
        [(ids[:, k : k + 1] == rows).astype(F32).astype(BF16) for k in range(n, n + count)], axis=0
    )
    return jnp.dot(pick, table[...], preferred_element_type=F32)


def lay_out(picked, n, count, coeffs, carry, store):
    bins = picked.shape[0] // count
    lane = lax.broadcasted_iota(jnp.int32, (bins, LANES), 1)
    for k in range(n, n + count):
        one = picked[bins * (k - n) : bins * (k - n + 1)]
        tile, shift = divmod(k * coeffs, LANES)
        first, second = one[:, :LANES], one[:, LANES:]
        if shift:
            first, second = pltpu.roll(first, shift, 1), pltpu.roll(second, shift, 1)
            before = lane < shift
            start = jnp.where(before, carry, first)
            middle = jnp.where(before, first, second)
            end = jnp.where(before, second, 0.0)
        else:
            start, middle, end = first, second, None
        store(tile, start)
        if shift + coeffs >= 2 * LANES:
            store(tile + 1, middle)
            carry = end
        else:
            carry = middle
    return carry


def rest_kernel(tops, coeffs, got, leaf, lists, rest_out, rows, table):
    doms = got.shape[0]
    bins, entries = lists.shape
    rows[...] = got[...].astype(F32)
    for s in range(SENT):
        table[doms * s : doms * (s + 1), :LANES] = rows[:, 8 + s, :].astype(BF16)
        end = rows[:, 14, :] if s == 3 else rows[:, 13, :]
        if 0 < s < 3:
            end = pltpu.roll(end, LANES - s * END, 1)
        table[doms * s : doms * (s + 1), LANES:] = end.astype(BF16)
    used = doms * SENT
    table[used : used + bins] = leaf[...]
    used += bins
    table[used:] = jnp.zeros((table.shape[0] - used, WIDTH), BF16)
    ids = lists[...]

    def store(tile, value):
        rest_out[:, LANES * tile : LANES * (tile + 1)] = value.astype(BF16)

    carry = None
    for n in range(0, entries, 8):
        carry = lay_out(picked_rows(ids, tops, table, n, 8), n, 8, coeffs, carry, store)


def rest_call(tops, coeffs, got, leaf, lists):
    bins, entries = lists.shape
    table_rows = -(-(SENT * got.shape[0] + bins) // 256) * 256
    return pl.pallas_call(
        functools.partial(rest_kernel, tops, coeffs),
        out_shape=pltpu.VMEM((bins, entries * coeffs), BF16),
        in_specs=[VMEM] * 3,
        out_specs=VMEM,
        scratch_shapes=[pltpu.VMEM(got.shape, F32), pltpu.VMEM((table_rows, WIDTH), BF16)],
        compiler_params=pltpu.CompilerParams(vmem_limit_bytes=8 * 2**20),
        cost_estimate=pl.CostEstimate(flops=1_000_000_000, bytes_accessed=2_000_000, transcendentals=0),
        name="rest",
    )(got, leaf, lists)


def far_kernel(mine, other, rest, lists, ops, placing, wide, out, table, far_cols, local_rows, flat, held, arrived):
    bins, entries = lists.shape
    coeffs = ops.shape[0]
    span = ops.shape[1] // PIECES
    copies = [
        pltpu.make_async_copy(
            ops.at[:, span * n : span * (n + 1)], held.at[:, span * n : span * (n + 1)], arrived.at[n]
        )
        for n in range(PIECES)
    ]
    for copy in copies:
        copy.start()
    layers, doms = mine.shape[0], mine.shape[1] * 2 // 3
    half = doms // 2
    for z in range(2 * layers):
        from_core, layer = (mine, z) if z < layers else (other, z - layers)
        table[doms * z : doms * (z + 1), :LANES] = from_core[layer, :doms, :]
        ends = from_core[layer, doms:, :]
        table[doms * z : doms * z + half, LANES:] = ends
        table[doms * z + half : doms * (z + 1), LANES:] = pltpu.roll(ends.astype(F32), LANES // 2, 1).astype(BF16)
    ids = lists[...]

    def store(tile, value):
        columns = slice(LANES * tile, LANES * (tile + 1))
        flat[:, columns] = (value + rest[:, columns].astype(F32)).astype(BF16)

    local = None
    carry = None
    done = 0
    for n in range(0, entries, 8):
        carry = lay_out(picked_rows(ids, 0, table, n, 8), n, 8, coeffs, carry, store)
        ready = (n + 8) * coeffs // LANES * LANES
        while done < PIECES and span * (done + 1) <= ready:
            columns = slice(span * done, span * (done + 1))
            copies[done].wait()
            term = lax.dot_general(
                flat[:, columns], held[:, columns], (((1,), (1,)), ((), ())), preferred_element_type=F32
            )
            local = term if local is None else local + term
            done += 1
    local = jnp.concatenate([local, jnp.zeros((bins, WIDTH - coeffs), F32)], axis=1)
    spread = None
    rest = local
    for _ in range(3):
        piece = rest.astype(BF16)
        rest = rest - piece.astype(F32)
        term = lax.dot_general(placing[...], piece, (((1,), (1,)), ((), ())), preferred_element_type=F32)
        spread = term if spread is None else spread + term
    local_rows[...] = jnp.concatenate([spread[SLOTS * j : SLOTS * (j + 1)] for j in range(4)], axis=1)
    lane_group = lax.div(lax.broadcasted_iota(jnp.int32, (8, LANES), 1), bins)

    def step(i, carry):
        series = []
        for half in range(2):
            at = pl.ds(pl.multiple_of(16 * i + 8 * half, 8), 8)
            tx = chebyshev(wide[0, at, :])
            ty = chebyshev(wide[1, at, :])
            tz = grouped(chebyshev(wide[2, at, :]), lane_group)
            series.append((at, tx, ty, tz))
        totals = [None, None]
        g = 0
        while g < len(GROUPS):
            ax, ay, _ = GROUPS[g]
            inner = [None, None]
            while g < len(GROUPS) and GROUPS[g][:2] == (ax, ay):
                row = local_rows[g : g + 1, :]
                for h in range(2):
                    value = series[h][3][GROUPS[g][2]] * row
                    inner[h] = value if inner[h] is None else inner[h] + value
                g += 1
            for h in range(2):
                _, tx, ty, _ = series[h]
                value = inner[h]
                if ax:
                    value = value * tx[ax]
                if ay:
                    value = value * ty[ay]
                totals[h] = value if totals[h] is None else totals[h] + value
        for h in range(2):
            far_cols[series[h][0], :] = totals[h]
        return carry

    lax.fori_loop(0, 8, step, 0)
    spread_far = far_cols[...].T
    far = spread_far[:bins]
    for j in range(1, 4):
        far = far + spread_far[bins * j : bins * (j + 1)]
    out[...] = far


def far_call(mine, other, rest, lists, ops, placing, wide):
    bins = lists.shape[0]
    table_rows = 2 * mine.shape[0] * mine.shape[1] * 2 // 3
    return pl.pallas_call(
        far_kernel,
        out_shape=pltpu.VMEM((bins, LANES), F32),
        in_specs=[VMEM] * 4 + [HBM] + [VMEM] * 2,
        out_specs=VMEM,
        scratch_shapes=[
            pltpu.VMEM((table_rows, WIDTH), BF16),
            pltpu.VMEM((LANES, LANES), F32),
            pltpu.VMEM((SLOTS, LANES), F32),
            pltpu.VMEM((bins, ops.shape[1]), BF16),
            pltpu.VMEM(ops.shape, BF16),
            pltpu.SemaphoreType.DMA((PIECES,)),
        ],
        compiler_params=pltpu.CompilerParams(vmem_limit_bytes=16 * 2**20),
        cost_estimate=pl.CostEstimate(flops=5_000_000_000, bytes_accessed=12_000_000, transcendentals=0),
        name="far",
    )(mine, other, rest, lists, pltpu.with_memory_space_constraint(ops, pltpu.HBM), placing, wide)


def shards(positions, masses, fill, translations, m2l_lists, cell_sends, bin_sends, task_target, task_source, task_offset):
    pos = jnp.transpose(positions[0, 0], (1, 0, 2))
    mass = masses[0, 0]
    fill_row = fill[0]
    cells = cell_sends[0, 0].T
    sends = bin_sends.reshape(1, -1)
    placing = jnp.asarray(placing_matrix(), BF16)
    doms = cells.shape[1]
    layers = lax.axis_size("z")
    core = lax.axis_index("core").astype(jnp.int32).reshape(1)
    leaf, live_mass, wide, cast = moments_call(pos, mass, fill_row, cells, sends, placing)
    got = lax.all_to_all(cast, "dom", split_axis=0, concat_axis=0, tiled=True)
    pos, ids, placing, target, source, offset, sends, staged = stage_call(
        core, layers * lax.axis_size("core"), live_mass,
        pos, m2l_lists[0, 0], placing, task_target[0], task_source[0], task_offset[0], sends,
    )
    layered, ready = spread_call(got, staged, layers)
    column = lax.all_to_all(layered, "z", split_axis=0, concat_axis=0, tiled=True)
    near, back = near_call(pos, live_mass, got, target, source, offset, ready)
    rest = rest_call(layers * lax.axis_size("core") * doms, translations.shape[0], got, leaf, ids)
    column, near, back, rest = lax.optimization_barrier((column, near, back, rest))
    returned = lax.all_to_all(back.reshape(doms, 1, LANES), "dom", split_axis=0, concat_axis=0, tiled=True)
    other = lax.ppermute(column, "core", [(0, 1), (1, 0)])
    far = far_call(column, other, rest, ids, translations, placing, wide)
    far, near, returned = lax.optimization_barrier((far, near, returned))
    homing = (jnp.arange(mass.shape[0], dtype=jnp.int32)[:, None] == bin_sends.reshape(1, -1)).astype(F32)
    home = jnp.dot(homing, returned.reshape(doms, LANES), precision=lax.Precision.HIGHEST)
    live = jnp.arange(LANES, dtype=jnp.int32)[None, :] < fill[0, 0][:, None]
    out = jnp.where(live, far + near + home, 0.0)
    return out[None, None]


def solution(mesh):
    regions, doms = mesh.devices.shape
    cores = 2
    split = jax.sharding.Mesh(mesh.devices.reshape(regions // cores, cores, doms), ("z", "core", "dom"))

    def at(*rest):
        return P(("z", "core"), "dom", *rest)

    return jax.shard_map(
        shards,
        mesh=split,
        in_specs=(at(), at(), at(), P(), at(), at(), at(), at(), at(), at()),
        out_specs=at(),
        check_vma=False,
    )
```

```python
import functools
import jax
import jax.numpy as jnp
import numpy as np
from jax import lax
from jax.experimental import pallas as pl
from jax.experimental.pallas import tpu as pltpu
from jax.sharding import PartitionSpec as P

ORDER = 8
SOFTENING = 0.01
LANES = 128
WIDTH = 256
PIECES = 5
SENT = 4
END = 40
SLOTS = 64
F32 = jnp.float32
BF16 = jnp.bfloat16
VMEM = pl.BlockSpec(memory_space=pltpu.VMEM)
HBM = pl.BlockSpec(memory_space=pltpu.HBM)
SMEM = pl.BlockSpec(memory_space=pltpu.SMEM)


def coefficient_groups():
    groups = []
    for ax in range(ORDER + 1):
        for ay in range(ORDER + 1 - ax):
            for part in range((ORDER - ax - ay) // 4 + 1):
                groups.append((ax, ay, part))
    return groups


GROUPS = coefficient_groups()


def placing_matrix():
    index, at = {}, 0
    for total in range(ORDER + 1):
        for ax in range(total, -1, -1):
            for ay in range(total - ax, -1, -1):
                index[(ax, ay, total - ax - ay)] = at
                at += 1
    placing = np.zeros((WIDTH, WIDTH), np.float32)
    for row, (ax, ay, part) in enumerate(GROUPS):
        for j in range(4):
            place = index.get((ax, ay, 4 * part + j))
            if place is not None:
                placing[j * SLOTS + row, place] = 1.0
    return placing


def chebyshev(t):
    series = [jnp.ones_like(t), t]
    for _ in range(2, ORDER + 1):
        series.append(2.0 * t * series[-1] - series[-2])
    return series


def grouped(series, lane_group):
    parts = []
    for n in range(3):
        value = series[4 * n]
        for j in range(1, 4):
            other = series[4 * n + j] if 4 * n + j <= ORDER else jnp.zeros_like(value)
            value = jnp.where(lane_group == j, other, value)
        parts.append(value)
    return parts


def four_wide(rows):
    return jnp.concatenate([rows] * 4, axis=0).T


def live_rows(fill_row, masses):
    bins, slots = masses.shape
    eye = lax.broadcasted_iota(jnp.int32, (bins, bins), 0) == lax.broadcasted_iota(
        jnp.int32, (bins, bins), 1
    )
    fill_col = jnp.sum(
        jnp.where(eye, fill_row.astype(F32), 0.0), axis=1, keepdims=True
    )
    slot = lax.broadcasted_iota(jnp.int32, (bins, slots), 1).astype(F32)
    return slot < fill_col


def moments_kernel(pos, mass, fill, cells, sends, placing, leaf_out, live_out, wide, cast_out, acc, rows):
    bins = mass.shape[0]
    live_mass = jnp.where(live_rows(fill[...], mass[...]), mass[...], 0.0)
    live_out[...] = live_mass
    for c in range(3):
        wide[c] = four_wide(pos[c])
    wide[3] = four_wide(live_mass)
    acc[...] = jnp.zeros_like(acc)
    lane_group = lax.div(lax.broadcasted_iota(jnp.int32, (8, LANES), 1), bins)

    def step(i, carry):
        sums = [None] * len(GROUPS)
        for half in range(2):
            at = pl.ds(pl.multiple_of(16 * i + 8 * half, 8), 8)
            tx = chebyshev(wide[0, at, :])
            ty = chebyshev(wide[1, at, :])
            m = wide[3, at, :]
            tz = [v * m for v in grouped(chebyshev(wide[2, at, :]), lane_group)]
            last = None
            for g, (ax, ay, part) in enumerate(GROUPS):
                if last is None or last[0] != (ax, ay):
                    last = ((ax, ay), tx[ax] * ty[ay] if ax and ay else (tx[ax] if ax else ty[ay]))
                value = last[1] * tz[part] if (ax or ay) else tz[part]
                sums[g] = value if sums[g] is None else sums[g] + value
        for g in range(len(GROUPS)):
            acc[g] += sums[g]
        return carry

    lax.fori_loop(0, 8, step, 0)
    raw = jnp.sum(acc[...], axis=1).T
    moments = jnp.concatenate([raw[bins * j : bins * (j + 1)] for j in range(4)], axis=1)
    top = jnp.sum(moments, axis=0, keepdims=True) * (1.0 / bins)
    both = jnp.concatenate([moments, jnp.broadcast_to(top, (cells.shape[1], WIDTH))], axis=0).astype(BF16)
    placed = jnp.dot(both, placing[...], preferred_element_type=F32)
    leaf = placed[:bins].astype(BF16)
    leaf_out[...] = leaf
    doms = cells.shape[1]
    rows[:, 12, :] = placed[bins:, :LANES]
    ends = [placed[bins:, LANES:]]
    for s in range(SENT):
        pick = (lax.broadcasted_iota(jnp.int32, (bins, doms), 0) == cells[s : s + 1, :]).astype(F32).astype(BF16)
        one = lax.dot_general(pick, leaf, (((0,), (0,)), ((), ())), preferred_element_type=F32)
        rows[:, 8 + s, :] = one[:, :LANES]
        ends.append(one[:, LANES:])
    rows[:, 13, :] = ends[1] + pltpu.roll(ends[2], END, 1) + pltpu.roll(ends[3], 2 * END, 1)
    rows[:, 14, :] = ends[4] + pltpu.roll(ends[0], END, 1)
    rows[:, 15, :] = jnp.zeros((doms, LANES), F32)
    for d in range(doms):
        b = sends[0, d]
        for c in range(3):
            rows[d, c : c + 1, :] = pos[c, pl.ds(b, 1), :]
        rows[d, 3:4, :] = live_out[pl.ds(b, 1), :]
    value = rows[:, 0:4, :]
    rows[:, 4:8, :] = value - value.astype(BF16).astype(F32)
    cast_out[...] = rows[...].astype(BF16)


def moments_call(pos, mass, fill, cells, sends, placing):
    bins, doms = mass.shape[0], cells.shape[1]
    return pl.pallas_call(
        moments_kernel,
        out_shape=(
            pltpu.VMEM((bins, WIDTH), BF16),
            pltpu.VMEM((bins, LANES), F32),
            pltpu.VMEM((4, LANES, LANES), F32),
            pltpu.VMEM((doms, 16, LANES), BF16),
        ),
        in_specs=[VMEM] * 4 + [SMEM, VMEM],
        out_specs=(VMEM,) * 4,
        scratch_shapes=[
            pltpu.VMEM((SLOTS, 8, LANES), F32),
            pltpu.VMEM((doms, 16, LANES), F32),
        ],
        cost_estimate=pl.CostEstimate(flops=6_000_000, bytes_accessed=600_000, transcendentals=0),
        name="moments",
    )(pos, mass, fill, cells, sends, placing)


def stage_kernel(core, regions, pos, lists, placing, target, source, offset, sends, after, *rest):
    ins = (pos, lists, placing, target, source, offset, sends)
    outs, token, arrived = rest[: len(ins)], rest[-2], rest[-1]
    copies = [pltpu.make_async_copy(a, b, arrived.at[n]) for n, (a, b) in enumerate(zip(ins, outs))]
    for copy in copies:
        copy.start()
    token[...] = after[0:8, :]
    for copy in copies:
        copy.wait()
    ids = outs[1][...]
    doms = sends.shape[1]
    half = regions // 2 * doms
    tops = 2 * half
    region = lax.div(ids, doms)
    cell = ids - tops
    outs[1][...] = jnp.where(
        ids < tops,
        ((region & 1) ^ core[0]) * half + lax.div(region, 2) * doms + lax.rem(ids, doms),
        jnp.where(cell < doms * SENT, tops + lax.rem(cell, SENT) * doms + lax.div(cell, SENT), ids),
    )


def stage_call(core, regions, after, *arrays):
    def kernel(core_ref, *refs):
        stage_kernel(core_ref, regions, *refs)

    return pl.pallas_call(
        kernel,
        out_shape=tuple(pltpu.VMEM(a.shape, a.dtype) for a in arrays) + (pltpu.VMEM((8, LANES), F32),),
        in_specs=[SMEM] + [HBM] * len(arrays) + [VMEM],
        out_specs=(VMEM,) * (len(arrays) + 1),
        scratch_shapes=[pltpu.SemaphoreType.DMA((len(arrays),))],
        compiler_params=pltpu.CompilerParams(vmem_limit_bytes=4 * 2**20),
        cost_estimate=pl.CostEstimate(flops=0, bytes_accessed=1_000_000, transcendentals=0),
        name="stage",
    )(core, *[pltpu.with_memory_space_constraint(a, pltpu.HBM) for a in arrays], after)


def spread_kernel(got, after, out, token):
    token[...] = after[...]
    rows = got[...].astype(F32)
    doms = got.shape[0]
    half = doms // 2
    first = rows[:, 12, :].astype(BF16)
    end = pltpu.roll(rows[:, 14, :], LANES - END, 1)
    lane = lax.broadcasted_iota(jnp.int32, (half, LANES), 1)
    ends = jnp.where(lane < LANES // 2, end[:half], pltpu.roll(end[half:], LANES // 2, 1)).astype(BF16)
    for z in range(out.shape[0]):
        out[z, :doms, :] = first
        out[z, doms:, :] = ends


def spread_call(got, after, layers):
    return pl.pallas_call(
        spread_kernel,
        out_shape=(pltpu.VMEM((layers, got.shape[0] * 3 // 2, LANES), BF16), pltpu.VMEM((8, LANES), F32)),
        in_specs=[VMEM, VMEM],
        out_specs=(VMEM, VMEM),
        compiler_params=pltpu.CompilerParams(vmem_limit_bytes=4 * 2**20),
        cost_estimate=pl.CostEstimate(flops=0, bytes_accessed=600_000, transcendentals=0),
        name="spread",
    )(got, after)


def near_kernel(pos, live_mass, got, target, source, offset, after, near_out, back_out, rows, wide, acc):
    own = live_mass.shape[0]
    total = rows.shape[0]
    for c in range(3):
        rows[:own, c, :] = pos[c]
    rows[:own, 3, :] = live_mass[...]
    arrived = got[...].astype(F32)
    rows[own:, 0:4, :] = arrived[:, 0:4, :] + arrived[:, 4:8, :]
    rows[:, 4:, :] = jnp.zeros((total, 4, LANES), F32)
    acc[...] = jnp.zeros_like(acc)
    part = lax.broadcasted_iota(jnp.int32, (32, 4 * LANES), 0)
    lane = lax.broadcasted_iota(jnp.int32, (32, 4 * LANES), 1)
    repeat = jnp.logical_and((part & 7) == lax.div(lane, LANES), part < 24).astype(F32).astype(BF16)

    def turn(b, carry):
        value = rows[b]
        high = value.astype(BF16)
        rest = value - high.astype(F32)
        middle = rest.astype(BF16)
        low = rest - middle.astype(F32)
        parts = jnp.concatenate(
            [high.astype(F32), middle.astype(F32), low, jnp.zeros_like(value)], axis=0
        ).astype(BF16)
        wide[b] = lax.dot_general(
            parts, repeat, (((0,), (0,)), ((), ())), preferred_element_type=F32
        )
        return carry

    lax.fori_loop(0, total, turn, 0, unroll=32)

    def task(t, carry):
        i, j, o = target[0, t], source[0, t], offset[0, t]
        sx = 2.0 * (lax.div(o, 9) - 1).astype(F32)
        sy = 2.0 * (lax.rem(lax.div(o, 3), 3) - 1).astype(F32)
        sz = 2.0 * (lax.rem(o, 3) - 1).astype(F32)
        tx = rows[i, 0:1, :] - sx
        ty = rows[i, 1:2, :] - sy
        tz = rows[i, 2:3, :] - sz
        parts = []
        for n in range(LANES // 8):
            q = slice(8 * n, 8 * n + 8)
            dx = wide[j, q, :LANES] - tx
            dy = wide[j, q, LANES : 2 * LANES] - ty
            dz = wide[j, q, 2 * LANES : 3 * LANES] - tz
            d = (dx * dx + SOFTENING) + dy * dy + dz * dz
            parts.append(wide[j, q, 3 * LANES :] * lax.rsqrt(d))
        while len(parts) > 1:
            parts = [a + b for a, b in zip(parts[::2], parts[1::2])]
        same = jnp.logical_and(i == j, o == 13).astype(F32)
        own_term = (same * 0.125) * (rows[i, 3:4, :] * lax.rsqrt(jnp.full((1, LANES), SOFTENING, F32)))
        acc[i] += parts[0] - own_term
        return carry

    lax.fori_loop(0, target.shape[1], task, 0, unroll=8)
    near = jnp.sum(acc[...], axis=1)
    near_out[...] = near[:own]
    back_out[...] = near[own:]


def near_call(pos, live_mass, got, target, source, offset, after):
    own = live_mass.shape[0]
    total = own + got.shape[0]
    return pl.pallas_call(
        near_kernel,
        out_shape=(pltpu.VMEM((own, LANES), F32), pltpu.VMEM((total - own, LANES), F32)),
        in_specs=[VMEM, VMEM, VMEM, SMEM, SMEM, SMEM, VMEM],
        out_specs=(VMEM, VMEM),
        cost_estimate=pl.CostEstimate(flops=26_000_000, bytes_accessed=600_000, transcendentals=2_000_000),
        scratch_shapes=[
            pltpu.VMEM((total, 8, LANES), F32),
            pltpu.VMEM((total, LANES, 4 * LANES), F32),
            pltpu.VMEM((total, 8, LANES), F32),
        ],
        compiler_params=pltpu.CompilerParams(vmem_limit_bytes=20 * 2**20),
        name="near",
    )(pos, live_mass, got, target, source, offset, after)


def picked_rows(ids, first, table, n, count):
    rows = lax.broadcasted_iota(jnp.int32, (ids.shape[0], table.shape[0]), 1) + first
    pick = jnp.concatenate(
        [(ids[:, k : k + 1] == rows).astype(F32).astype(BF16) for k in range(n, n + count)], axis=0
    )
    return jnp.dot(pick, table[...], preferred_element_type=F32)


def lay_out(picked, n, count, coeffs, carry, store):
    bins = picked.shape[0] // count
    lane = lax.broadcasted_iota(jnp.int32, (bins, LANES), 1)
    for k in range(n, n + count):
        one = picked[bins * (k - n) : bins * (k - n + 1)]
        tile, shift = divmod(k * coeffs, LANES)
        first, second = one[:, :LANES], one[:, LANES:]
        if shift:
            first, second = pltpu.roll(first, shift, 1), pltpu.roll(second, shift, 1)
            before = lane < shift
            start = jnp.where(before, carry, first)
            middle = jnp.where(before, first, second)
            end = jnp.where(before, second, 0.0)
        else:
            start, middle, end = first, second, None
        store(tile, start)
        if shift + coeffs >= 2 * LANES:
            store(tile + 1, middle)
            carry = end
        else:
            carry = middle
    return carry


def rest_kernel(tops, coeffs, got, leaf, lists, rest_out, rows, table):
    doms = got.shape[0]
    bins, entries = lists.shape
    rows[...] = got[...].astype(F32)
    for s in range(SENT):
        table[doms * s : doms * (s + 1), :LANES] = rows[:, 8 + s, :].astype(BF16)
        end = rows[:, 14, :] if s == 3 else rows[:, 13, :]
        if 0 < s < 3:
            end = pltpu.roll(end, LANES - s * END, 1)
        table[doms * s : doms * (s + 1), LANES:] = end.astype(BF16)
    used = doms * SENT
    table[used : used + bins] = leaf[...]
    used += bins
    table[used:] = jnp.zeros((table.shape[0] - used, WIDTH), BF16)
    ids = lists[...]

    def store(tile, value):
        rest_out[:, LANES * tile : LANES * (tile + 1)] = value.astype(BF16)

    carry = None
    for n in range(0, entries, 8):
        carry = lay_out(picked_rows(ids, tops, table, n, 8), n, 8, coeffs, carry, store)


def rest_call(tops, coeffs, got, leaf, lists):
    bins, entries = lists.shape
    table_rows = -(-(SENT * got.shape[0] + bins) // 256) * 256
    return pl.pallas_call(
        functools.partial(rest_kernel, tops, coeffs),
        out_shape=pltpu.VMEM((bins, entries * coeffs), BF16),
        in_specs=[VMEM] * 3,
        out_specs=VMEM,
        scratch_shapes=[pltpu.VMEM(got.shape, F32), pltpu.VMEM((table_rows, WIDTH), BF16)],
        compiler_params=pltpu.CompilerParams(vmem_limit_bytes=8 * 2**20),
        cost_estimate=pl.CostEstimate(flops=1_000_000_000, bytes_accessed=2_000_000, transcendentals=0),
        name="rest",
    )(got, leaf, lists)


def far_kernel(mine, other, rest, lists, ops, placing, wide, out, table, far_cols, local_rows, flat, held, arrived):
    bins, entries = lists.shape
    coeffs = ops.shape[0]
    span = ops.shape[1] // PIECES
    copies = [
        pltpu.make_async_copy(
            ops.at[:, span * n : span * (n + 1)], held.at[:, span * n : span * (n + 1)], arrived.at[n]
        )
        for n in range(PIECES)
    ]
    for copy in copies:
        copy.start()
    layers, doms = mine.shape[0], mine.shape[1] * 2 // 3
    half = doms // 2
    for z in range(2 * layers):
        from_core, layer = (mine, z) if z < layers else (other, z - layers)
        table[doms * z : doms * (z + 1), :LANES] = from_core[layer, :doms, :]
        ends = from_core[layer, doms:, :]
        table[doms * z : doms * z + half, LANES:] = ends
        table[doms * z + half : doms * (z + 1), LANES:] = pltpu.roll(ends.astype(F32), LANES // 2, 1).astype(BF16)
    ids = lists[...]

    def store(tile, value):
        columns = slice(LANES * tile, LANES * (tile + 1))
        flat[:, columns] = (value + rest[:, columns].astype(F32)).astype(BF16)

    local = None
    carry = None
    done = 0
    for n in range(0, entries, 8):
        carry = lay_out(picked_rows(ids, 0, table, n, 8), n, 8, coeffs, carry, store)
        ready = (n + 8) * coeffs // LANES * LANES
        while done < PIECES and span * (done + 1) <= ready:
            columns = slice(span * done, span * (done + 1))
            copies[done].wait()
            term = lax.dot_general(
                flat[:, columns], held[:, columns], (((1,), (1,)), ((), ())), preferred_element_type=F32
            )
            local = term if local is None else local + term
            done += 1
    local = jnp.concatenate([local, jnp.zeros((bins, WIDTH - coeffs), F32)], axis=1)
    spread = None
    rest = local
    for _ in range(3):
        piece = rest.astype(BF16)
        rest = rest - piece.astype(F32)
        term = lax.dot_general(placing[...], piece, (((1,), (1,)), ((), ())), preferred_element_type=F32)
        spread = term if spread is None else spread + term
    local_rows[...] = jnp.concatenate([spread[SLOTS * j : SLOTS * (j + 1)] for j in range(4)], axis=1)
    lane_group = lax.div(lax.broadcasted_iota(jnp.int32, (8, LANES), 1), bins)

    def step(i, carry):
        series = []
        for half in range(2):
            at = pl.ds(pl.multiple_of(16 * i + 8 * half, 8), 8)
            tx = chebyshev(wide[0, at, :])
            ty = chebyshev(wide[1, at, :])
            tz = grouped(chebyshev(wide[2, at, :]), lane_group)
            series.append((at, tx, ty, tz))
        totals = [None, None]
        g = 0
        while g < len(GROUPS):
            ax, ay, _ = GROUPS[g]
            inner = [None, None]
            while g < len(GROUPS) and GROUPS[g][:2] == (ax, ay):
                row = local_rows[g : g + 1, :]
                for h in range(2):
                    value = series[h][3][GROUPS[g][2]] * row
                    inner[h] = value if inner[h] is None else inner[h] + value
                g += 1
            for h in range(2):
                _, tx, ty, _ = series[h]
                value = inner[h]
                if ax:
                    value = value * tx[ax]
                if ay:
                    value = value * ty[ay]
                totals[h] = value if totals[h] is None else totals[h] + value
        for h in range(2):
            far_cols[series[h][0], :] = totals[h]
        return carry

    lax.fori_loop(0, 8, step, 0, unroll=2)
    spread_far = far_cols[...].T
    far = spread_far[:bins]
    for j in range(1, 4):
        far = far + spread_far[bins * j : bins * (j + 1)]
    out[...] = far


def far_call(mine, other, rest, lists, ops, placing, wide):
    bins = lists.shape[0]
    table_rows = 2 * mine.shape[0] * mine.shape[1] * 2 // 3
    return pl.pallas_call(
        far_kernel,
        out_shape=pltpu.VMEM((bins, LANES), F32),
        in_specs=[VMEM] * 4 + [HBM] + [VMEM] * 2,
        out_specs=VMEM,
        scratch_shapes=[
            pltpu.VMEM((table_rows, WIDTH), BF16),
            pltpu.VMEM((LANES, LANES), F32),
            pltpu.VMEM((SLOTS, LANES), F32),
            pltpu.VMEM((bins, ops.shape[1]), BF16),
            pltpu.VMEM(ops.shape, BF16),
            pltpu.SemaphoreType.DMA((PIECES,)),
        ],
        compiler_params=pltpu.CompilerParams(vmem_limit_bytes=16 * 2**20),
        cost_estimate=pl.CostEstimate(flops=5_000_000_000, bytes_accessed=12_000_000, transcendentals=0),
        name="far",
    )(mine, other, rest, lists, pltpu.with_memory_space_constraint(ops, pltpu.HBM), placing, wide)


def shards(positions, masses, fill, translations, m2l_lists, cell_sends, bin_sends, task_target, task_source, task_offset):
    pos = jnp.transpose(positions[0, 0], (1, 0, 2))
    mass = masses[0, 0]
    fill_row = fill[0]
    cells = cell_sends[0, 0].T
    sends = bin_sends.reshape(1, -1)
    placing = jnp.asarray(placing_matrix(), BF16)
    doms = cells.shape[1]
    layers = lax.axis_size("z")
    core = lax.axis_index("core").astype(jnp.int32).reshape(1)
    leaf, live_mass, wide, cast = moments_call(pos, mass, fill_row, cells, sends, placing)
    got = lax.all_to_all(cast, "dom", split_axis=0, concat_axis=0, tiled=True)
    pos, ids, placing, target, source, offset, sends, staged = stage_call(
        core, layers * lax.axis_size("core"), live_mass,
        pos, m2l_lists[0, 0], placing, task_target[0], task_source[0], task_offset[0], sends,
    )
    layered, ready = spread_call(got, staged, layers)
    column = lax.all_to_all(layered, "z", split_axis=0, concat_axis=0, tiled=True)
    near, back = near_call(pos, live_mass, got, target, source, offset, ready)
    rest = rest_call(layers * lax.axis_size("core") * doms, translations.shape[0], got, leaf, ids)
    column, near, back, rest = lax.optimization_barrier((column, near, back, rest))
    returned = lax.all_to_all(back.reshape(doms, 1, LANES), "dom", split_axis=0, concat_axis=0, tiled=True)
    other = lax.ppermute(column, "core", [(0, 1), (1, 0)])
    far = far_call(column, other, rest, ids, translations, placing, wide)
    far, near, returned = lax.optimization_barrier((far, near, returned))
    homing = (jnp.arange(mass.shape[0], dtype=jnp.int32)[:, None] == bin_sends.reshape(1, -1)).astype(F32)
    home = jnp.dot(homing, returned.reshape(doms, LANES), precision=lax.Precision.HIGHEST)
    live = jnp.arange(LANES, dtype=jnp.int32)[None, :] < fill[0, 0][:, None]
    out = jnp.where(live, far + near + home, 0.0)
    return out[None, None]


def solution(mesh):
    regions, doms = mesh.devices.shape
    cores = 2
    split = jax.sharding.Mesh(mesh.devices.reshape(regions // cores, cores, doms), ("z", "core", "dom"))

    def at(*rest):
        return P(("z", "core"), "dom", *rest)

    return jax.shard_map(
        shards,
        mesh=split,
        in_specs=(at(), at(), at(), P(), at(), at(), at(), at(), at(), at()),
        out_specs=at(),
        check_vma=False,
    )
```
